32 devices in a mesh: groups: 2 (over y), row: 16 (over z, x, core).
Axes of the slice: x: 2, y: 2, z: 4, core: 2. Of those that a mesh axis runs over, the one named last changes fastest.
Arguments:
- b3_store: bfloat16 [384, 5, 68, 576], P(('groups', 'row')), parts along dimension 0, may hold values from -1.1953125 to 1.1953125
- block_shift: int32 [24, 5], P('groups'), parts along dimension 0, may hold values from 0 to 15, as said below
- green: bfloat16 [2, 2, 384, 5, 576], P(None, None, ('groups', 'row')), parts along dimension 2, may hold values from -0.4 to 1.4, as said below
- block_mask: int32 [384, 5], P(('groups', 'row')), parts along dimension 0, may hold values 0 or 1
Outputs:
- chi_blocks: float32 [2, 384, 5, 4624], P(None, ('groups', 'row')), parts along dimension 1
The draws below stay inside these ranges and needn't reach their ends.
There are 2 independent parts, one for each index of `groups`. The reference program is written for one: setup_inputs(seed, part) draws one part's arguments, and reference() takes and returns one part's arrays. A program takes and returns all parts, laid end to end along the dimension named above; each array names one. Nothing has to cross between parts.
Inputs may be any that keep to these rules, and one draw needn't show every extreme that they name: `block_shift`: no value is taken by more than 4 entries, and some value by exactly 4. green[k, t, m, s] is the transpose of the block green[k, t, (m + s - 2) mod 192, 4 - s].
All inputs are finite; a program needn't handle non-finite values. No bound on the sum of `block_mask` on one device may be relied on, other than what follows from the above.
Results may differ from the reference program's by a relative error of at most 0.0012.
Values may be sent and summed in bfloat16 or wider, within the bound.
No kernel may reach another device: no remote copies, remote signals or barrier semaphores. Data moves between devices by JAX's collectives and lax.ppermute only.
A program may use at most 192 MiB of HBM per device.

```python
import jax
import jax.numpy as jnp
from jax import lax

BO = 24
BA = 68
HALF = 2
NTAU = 2
MOL_DEV = 12
NN = 5
NW = 9
MOLS = 192
CAP = 4
N_ROW = 16


def draw_block_shift(key, part):
    key = jax.random.fold_in(key, 7)
    first_key, second_key = jax.random.split(key)
    block_count = MOL_DEV * NN
    ordering = jax.random.permutation(first_key, block_count).astype(jnp.int32)
    others = (jax.random.permutation(second_key, N_ROW - 2) + 1).astype(jnp.int32)
    values = jnp.concatenate([jnp.array([0, N_ROW - 1], jnp.int32), others])
    return values[ordering // CAP].reshape(MOL_DEV, NN).astype(jnp.int32)


def draw_green(key, part):
    key = jax.random.fold_in(key, 5)
    first_key, second_key = jax.random.split(key)
    shape = (2, NTAU, MOLS, NN, BO, BO)
    raw_blocks = jnp.clip(0.08 * jax.random.normal(first_key, shape, jnp.float32), -0.4, 0.4)
    molecule = jnp.arange(MOLS, dtype=jnp.int32)
    slot_ids = jnp.arange(NN, dtype=jnp.int32)
    partner = (molecule[:, None] + slot_ids[None, :] - HALF) % MOLS
    mirror = raw_blocks[:, :, partner, (2 * HALF - slot_ids)[None, :]]
    symmetric = 0.5 * (raw_blocks + jnp.swapaxes(mirror, -1, -2))
    diagonal_values = jax.random.uniform(second_key, (2, NTAU, MOLS, 1, BO, 1), jnp.float32, 0.3, 1.0)
    self_slot = (slot_ids == HALF).astype(jnp.float32)[:, None, None]
    diagonal = diagonal_values * jnp.eye(BO, dtype=jnp.float32) * self_slot
    return (symmetric + diagonal).reshape(2, NTAU, MOLS, NN, BO * BO).astype(jnp.bfloat16)


def set_ends(drawn, key, least, largest):
    longest = drawn.shape.index(max(drawn.shape))
    spots = []
    for shift in (0, 1):
        where = [jax.random.randint(jax.random.fold_in(key, axis), (), 0, length) for axis, length in enumerate(drawn.shape)]
        where[longest] = (where[longest] + shift) % drawn.shape[longest]
        spots.append(tuple(where))
    return drawn.at[spots[0]].set(least).at[spots[1]].set(largest)


def levels(stream_key, shape, cuts, low, largest):
    level, own = 1.0, jax.random.fold_in(stream_key, 6)
    for dim, shards_of in cuts:
        steps = jnp.exp(jax.random.uniform(jax.random.fold_in(own, dim), (shards_of,), jnp.float32, low / len(cuts), largest / len(cuts)))
        level = level * jnp.repeat(steps, shape[dim] // shards_of).reshape([-1 if axis == dim else 1 for axis in range(len(shape))])
    return level


def scatter_about(key, dims, deviation, limit, cuts=(), held_as=jnp.bfloat16):
    values = deviation * jax.random.normal(key, dims, jnp.float32)
    if cuts:
        values = values * levels(key, dims, cuts, -0.22, 0.18)
    return jnp.clip(values, -limit, limit).astype(held_as)


def setup_inputs(seed: int = 0, part: int = 0) -> dict:
    keys = jax.random.split(jax.random.key(seed), 5)
    part_keys = jax.random.split(jax.random.fold_in(keys[4], part), 5)
    b3_store = scatter_about(part_keys[0], (MOLS, NN, BA, BO * BO), 0.2, 1.1953125, ((0, 16),))
    block_shift = draw_block_shift(jax.random.fold_in(jax.random.fold_in(keys[4], part), 71), part)
    green = draw_green(jax.random.fold_in(jax.random.fold_in(keys[4], part), 71), part)
    block_mask = set_ends((jax.random.randint(part_keys[3], (MOLS, NN), 0, 4) < 3).astype(jnp.int32), jax.random.fold_in(part_keys[3], 1), 0, 1)
    return dict(b3_store=b3_store, block_shift=block_shift, green=green, block_mask=block_mask)


def reference(b3_store, block_shift, green, block_mask):
    molecules = b3_store.shape[0]
    slot_ids = jnp.arange(NN, dtype=jnp.int32)
    molecule = jnp.arange(molecules, dtype=jnp.int32)
    device = molecule // MOL_DEV
    local_index = molecule % MOL_DEV
    source = ((device[:, None] + block_shift[local_index]) % N_ROW) * MOL_DEV + local_index[:, None]
    weights = block_mask.astype(jnp.float32)

    def blocks_of(target):
        source_rows = source[target]
        picked = b3_store[source_rows, slot_ids].astype(jnp.float32)
        return (picked * weights[target][:, None, None]).reshape(NN, BA, BO, BO)

    def single_molecule(target):
        own_blocks = blocks_of(target)
        neighbours = jax.vmap(blocks_of)((target + slot_ids - HALF) % molecules)
        results = []
        for time_point in range(NTAU):
            virtual_rows = green[1, time_point][(target + slot_ids - HALF) % molecules]
            virtual_rows = virtual_rows.astype(jnp.float32).reshape(NN, NN, BO, BO)
            spread = jnp.zeros((BA, BO, NW, BO), jnp.float32)
            for first in range(NN):
                for second in range(NN):
                    term = jnp.einsum('pmi,ij->pmj', own_blocks[first], virtual_rows[first, second])
                    spread = spread.at[:, :, first + second, :].add(term)
            spread = spread.astype(jnp.bfloat16).astype(jnp.float32)
            occupied_rows = green[0, time_point, target].astype(jnp.float32).reshape(NN, BO, BO)
            folded = jnp.einsum('pmvj,wml->pwlvj', spread, occupied_rows)
            folded = folded.astype(jnp.bfloat16).astype(jnp.float32)
            chi_list = []
            for slot in range(NN):
                window_part = folded[:, slot, :, slot:slot + NN, :]
                chi_list.append(jnp.einsum('pluj,uqlj->pq', window_part, neighbours[slot]).reshape(BA * BA))
            results.append(jnp.stack(chi_list))
        return jnp.stack(results)

    stacked = lax.map(single_molecule, molecule)
    return jnp.transpose(stacked, (1, 0, 2, 3))
```

```python
import functools

import jax
import jax.numpy as jnp
import numpy as np
from jax import lax
from jax.experimental import pallas as pl
from jax.experimental.pallas import tpu as pltpu
from jax.sharding import PartitionSpec as P

BO = 24
HALF = 2
NTAU = 2
NN = 5
NW = 9
LANE = 128
KEPT = 3
BF = jnp.bfloat16
F32 = jnp.float32
VMEM_LIMIT = 56 * 1024 * 1024


def call(body, name, grid, in_specs, out_specs, out_shape, scratch=(), prefetch=0):
    return pl.pallas_call(
        body,
        grid_spec=pltpu.PrefetchScalarGridSpec(
            num_scalar_prefetch=prefetch,
            grid=grid,
            in_specs=in_specs,
            out_specs=out_specs,
            scratch_shapes=list(scratch),
        ),
        out_shape=out_shape,
        name=name,
        compiler_params=pltpu.CompilerParams(vmem_limit_bytes=VMEM_LIMIT),
    )


def chunk_groups(aux):
    full = aux // 16
    last = [full] if aux % 16 else []
    return [list(range(full - 1)) + last, [full - 1]]


def piece_rows(groups, aux):
    return [min(16, aux - 16 * g) for g in groups]


def piece_starts(groups, aux, halves):
    starts, row = [], 0
    for height in piece_rows(groups, aux):
        starts.append(row)
        row += height * halves
    return starts, row


def pack_blocks(store, target, rank, devices, capacity, groups):
    count, aux, size = store.shape
    pair = 2 if capacity > 1 else 1
    halves = (capacity + pair - 1) // pair
    heights = piece_rows(groups, aux)
    starts, total = piece_starts(groups, aux, halves)
    steps = 4
    batch = count // steps

    def body(target_ref, rank_ref, *refs):
        out_ref = refs[-1]
        for i in range(batch):
            e = pl.program_id(0) * batch + i
            for r in range(halves * pair):

                @pl.when(rank_ref[e] == r)
                def _(i=i, e=e, r=r):
                    lanes = slice((r % pair) * size, (r % pair + 1) * size)
                    for ref, height, start in zip(refs, heights, starts):
                        first = start + (r // pair) * height
                        out_ref[target_ref[e], first : first + height, lanes] = ref[i, :height]

    shape = (devices, total, pair * size)
    return call(
        body,
        "pack_blocks",
        (steps,),
        [pl.BlockSpec((batch, 16, size), lambda i, *_, g=g: (i, g, 0)) for g in groups],
        pl.BlockSpec(shape, lambda i, *_: (0, 0, 0)),
        jax.ShapeDtypeStruct(shape, BF),
        prefetch=2,
    )(target, rank, *([store] * len(groups)))


def spread_out(incoming, source, rank, mask, molecules, aux, capacity, groups):
    size = BO * BO
    pair = 2 if capacity > 1 else 1
    halves = (capacity + pair - 1) // pair
    heights = piece_rows(groups, aux)
    starts, _ = piece_starts(groups, aux, halves)
    rows = 16 * len(groups)

    def body(source_ref, rank_ref, mask_ref, in_ref, out_ref, first_ref, last_ref):
        a = pl.program_id(0)
        for g, (height, start) in enumerate(zip(heights, starts)):
            blocks = []
            for s in range(NN):
                e = a * NN + s
                block = in_ref[source_ref[e], start : start + height, :]
                for h in range(1, halves):
                    other = in_ref[source_ref[e], start + h * height : start + (h + 1) * height, :]
                    block = jnp.where(rank_ref[e] // pair == h, other, block)
                own = block[:, :size]
                if pair == 2:
                    own = jnp.where(rank_ref[e] % pair == 1, block[:, size:], own)
                blocks.append(jnp.where(mask_ref[e] == 1, own, jnp.zeros_like(own)))
            gap = jnp.zeros((height, LANE - NN * BO), BF)
            if height < 16:
                out_ref[0, g * 16 : (g + 1) * 16] = jnp.zeros((16, BO * LANE), BF)
            for mu in range(BO):
                parts = [b[:, mu * BO : (mu + 1) * BO] for b in blocks] + [gap]
                out_ref[0, g * 16 : g * 16 + height, mu * LANE : (mu + 1) * LANE] = jnp.concatenate(
                    parts, axis=1
                )

        @pl.when(a < HALF)
        def _():
            first_ref[...] = out_ref[...]

        @pl.when(a >= molecules - HALF)
        def _():
            last_ref[...] = out_ref[...]

    shape = (1, rows, BO * LANE)
    return call(
        body,
        "spread_out",
        (molecules,),
        [pl.BlockSpec(incoming.shape, lambda a, *_: (0, 0, 0))],
        [
            pl.BlockSpec(shape, lambda a, *_: (a, 0, 0)),
            pl.BlockSpec(shape, lambda a, *_: (jnp.minimum(a, HALF - 1), 0, 0)),
            pl.BlockSpec(shape, lambda a, *_: (jnp.maximum(a - (molecules - HALF), 0), 0, 0)),
        ],
        [
            jax.ShapeDtypeStruct((molecules, *shape[1:]), BF),
            jax.ShapeDtypeStruct((HALF, *shape[1:]), BF),
            jax.ShapeDtypeStruct((HALF, *shape[1:]), BF),
        ],
        prefetch=3,
    )(source, rank, mask, incoming)


def fold_kernel(own, virtual, occupied, widen):
    molecules, rows = own.shape[:2]
    units = occupied.shape[0]

    def body(own_ref, virtual_ref, occ_ref, widen_ref, x_ref, window_ref):
        u = pl.program_id(0)
        a = jnp.where(u < molecules, u, u - molecules)

        def place(slots):
            for t in range(NTAU):
                for s in range(NN):
                    row = virtual_ref[t, a + s].astype(F32)
                    for k, w in enumerate(slots):
                        off = (s - w) * BO
                        if off >= 0:
                            parts = [jnp.zeros((BO, off), F32)] * (off > 0) + [
                                row[:, : NN * BO - off],
                                jnp.zeros((BO, LANE - NN * BO), F32),
                            ]
                        else:
                            parts = [row[:, -off:], jnp.zeros((BO, LANE - NN * BO - off), F32)]
                        lanes = slice((t * KEPT + k) * LANE, (t * KEPT + k + 1) * LANE)
                        window_ref[s * BO : (s + 1) * BO, lanes] = jnp.concatenate(parts, axis=1)

        @pl.when(u == 0)
        def _():
            window_ref[NN * BO :] = jnp.zeros((LANE - NN * BO, NTAU * KEPT * LANE), F32)

        @pl.when(u < molecules)
        def _():
            place((2, 3, 4))

        @pl.when(u >= molecules)
        def _():
            place((0, 1, 1))

        window = window_ref[...].astype(BF)
        krons = []
        shape = (KEPT * BO, 8, BO * 8)
        keep = lax.broadcasted_iota(jnp.int32, shape, 2) % 8 == lax.broadcasted_iota(jnp.int32, shape, 1)
        for t in range(NTAU):
            wide = jnp.dot(occ_ref[0, t], widen_ref[...], preferred_element_type=F32)
            wide = jnp.where(keep, jnp.broadcast_to(wide[:, None, :], shape), 0.0)
            krons.append(wide.reshape(KEPT * BO * 8, BO * 8).astype(BF))
        for g in range(rows // 16):
            own_rows = jnp.concatenate(
                [
                    own_ref[0, g * 16 : (g + 1) * 16, mu * LANE : (mu + 1) * LANE]
                    for mu in range(BO)
                ],
                axis=0,
            )
            spread = jnp.dot(own_rows, window, preferred_element_type=F32)
            for t in range(NTAU):
                first = t * rows + g * 16
                for w in range(KEPT):
                    lane = (t * KEPT + w) * LANE
                    part = spread[:, lane : lane + LANE].reshape(BO, 2, 8, LANE)
                    part = jnp.concatenate(
                        [part[:, 0].reshape(BO * 8, LANE), part[:, 1].reshape(BO * 8, LANE)],
                        axis=1,
                    ).astype(BF)
                    folded = jnp.dot(
                        krons[t][w * BO * 8 : (w + 1) * BO * 8], part, preferred_element_type=F32
                    ).reshape(BO, 8, 2 * LANE)
                    folded = jnp.concatenate(
                        [folded[:, :, :LANE], folded[:, :, LANE:]], axis=1
                    ).astype(BF)
                    for el in range(BO):
                        x_ref[0, w, first : first + 16, el * LANE : (el + 1) * LANE] = folded[el]

    whole = lambda x: pl.BlockSpec(x.shape, lambda u: (0,) * x.ndim)
    shape = (KEPT, NTAU * rows, BO * LANE)
    return call(
        body,
        "fold",
        (units,),
        [
            pl.BlockSpec((1, *own.shape[1:]), lambda u: (jnp.where(u < molecules, u, u - molecules), 0, 0)),
            whole(virtual),
            pl.BlockSpec((1, *occupied.shape[1:]), lambda u: (u, 0, 0, 0)),
            whole(widen),
        ],
        pl.BlockSpec((1, *shape), lambda u: (u, 0, 0, 0)),
        jax.ShapeDtypeStruct((units, *shape), BF),
        [pltpu.VMEM((LANE, NTAU * KEPT * LANE), F32)],
    )(own, virtual, occupied, widen)


def runs_of(groups):
    runs = []
    for at, g in enumerate(groups):
        if runs and runs[-1][1] + runs[-1][2] == g:
            runs[-1][2] += 1
        else:
            runs.append([at, g, 1])
    return runs


def chi_kernel(parts, folded, chunks, aux):
    molecules = parts[0][1].shape[0]
    total = molecules + 2 * HALF
    rows = sum(16 * len(groups) for groups in chunks)
    count = sum(len(p) for p in parts)
    moves = []
    for c, groups in enumerate(chunks):
        for which, (first, much) in enumerate(
            ((0, HALF), (HALF, molecules), (HALF + molecules, HALF))
        ):
            for at, g, length in runs_of(groups):
                moves.append((c * 3 + which, first, much, at * 16, g * 16, length * 16))
    plan = sorted((g, c, at) for c, groups in enumerate(chunks) for at, g in enumerate(groups))

    def body(*refs):
        ins, xs = refs[:count], refs[count : count + KEPT * len(chunks)]
        out_ref, blocks_ref, all_ref, sem = refs[count + KEPT * len(chunks) :]
        q = pl.program_id(0)

        def copies():
            for i, (which, first, much, at, to, length) in enumerate(moves):
                yield pltpu.make_async_copy(
                    ins[which].at[:, at : at + length],
                    blocks_ref.at[first : first + much, to : to + length],
                    sem.at[i],
                )

        @pl.when(q == 0)
        def _():
            for copy in copies():
                copy.start()
            for copy in copies():
                copy.wait()

        near = blocks_ref[q]
        chis = []
        for k in range(KEPT):
            results = [
                lax.dot_general(
                    xs[k * len(chunks) + c][0, 0], near, (((1,), (1,)), ((), ())),
                    preferred_element_type=F32,
                )
                for c in range(len(chunks))
            ]
            both = []
            for t in range(NTAU):
                pieces = []
                for _, c, at in plan:
                    first = t * 16 * len(chunks[c]) + at * 16
                    pieces.append(results[c][first : first + 16])
                both.append(jnp.concatenate(pieces, axis=0))
            chis.append(both)

        def put(back, w, values):
            ring_at = (q + 4 - back) % 4
            for t in range(NTAU):
                all_ref[ring_at, pl.ds((w * NTAU + t) * rows, rows), :rows] = values[t]

        flip = lambda both: [jnp.transpose(x) for x in both]

        @pl.when(q == 0)
        def _():
            put(-2, 0, chis[0])

        @pl.when(q == 1)
        def _():
            put(-1, 1, chis[1])
            put(-2, 0, chis[0])

        @pl.when(q >= 2)
        def _():
            put(0, 2, chis[0])

        @pl.when(q >= 3)
        def _():
            put(1, 3, chis[1])
            put(0, 1, flip(chis[1]))

        @pl.when(q >= 4)
        def _():
            put(2, 4, chis[2])
            put(0, 0, flip(chis[2]))
            mine = (q + 2) % 4
            flat = jnp.concatenate(
                [
                    all_ref[mine, pl.ds(p, NN * NTAU, stride=rows), :][:, :aux]
                    for p in range(aux)
                ],
                axis=1,
            )
            for w in range(NN):
                out_ref[0, w] = flat[w * NTAU : (w + 1) * NTAU]

    last = molecules - 1

    def unit(k):
        def index(q):
            at = jnp.clip(q - HALF - k, 0, last)
            if k == 0:
                at = jnp.where(q < HALF, molecules + q, at)
            if k == 1:
                at = jnp.where(q == 1, molecules, at)
            return at, k, 0, 0

        return index

    out = call(
        body,
        "chi",
        (total,),
        [pl.BlockSpec(memory_space=pl.ANY)] * count
        + [
            pl.BlockSpec((1, 1, *x.shape[2:]), unit(k)) for k in range(KEPT) for x in folded
        ],
        pl.BlockSpec((1, NN, NTAU, aux * aux), lambda q: (jnp.maximum(q - 2 * HALF, 0), 0, 0, 0)),
        jax.ShapeDtypeStruct((molecules, NN, NTAU, aux * aux), F32),
        [
            pltpu.VMEM((total, rows, BO * LANE), BF),
            pltpu.VMEM((4, NN * NTAU * rows, LANE), F32),
            pltpu.SemaphoreType.DMA((len(moves),)),
        ],
    )(*[x for p in parts for x in p], *(list(folded) * KEPT))
    return jnp.transpose(out, (2, 0, 1, 3))


def ring(low, high):
    count = lax.axis_size("row")
    up = [(i, (i + 1) % count) for i in range(count)]
    down = [(j, i) for i, j in up]
    return lax.ppermute(low, "row", up), lax.ppermute(high, "row", down)


def green_operands(green, below, above):
    mol_dev = green.shape[2]
    virtual = jnp.concatenate([below, green[1], above], axis=1)
    virtual = virtual.reshape(NTAU, mol_dev + 2 * HALF, NN, BO, BO)
    virtual = jnp.transpose(virtual, (0, 1, 3, 2, 4))
    virtual = virtual.reshape(NTAU, mol_dev + 2 * HALF, BO, NN * BO)
    occupied = green[0].reshape(NTAU, mol_dev, NN, BO, BO)
    first = occupied[:, :HALF]
    first = jnp.stack([first[:, :, 0], first[:, :, 1], first[:, :, 1]], axis=2)
    occupied = jnp.concatenate([occupied[:, :, HALF:], first], axis=1)
    occupied = jnp.transpose(occupied, (1, 0, 2, 4, 3))
    return virtual, occupied.reshape(mol_dev + HALF, NTAU, KEPT * BO, BO)


def shards(b3_store, block_shift, green, block_mask):
    devices = lax.axis_size("row")
    myself = lax.axis_index("row")
    mol_dev, _, aux, size = b3_store.shape
    count = mol_dev * NN
    capacity = (count + devices - 1) // devices
    pair = 2 if capacity > 1 else 1
    halves = (capacity + pair - 1) // pair
    shifts = block_shift.reshape(count)
    position = jnp.arange(count, dtype=jnp.int32)
    same = (shifts[:, None] == shifts[None, :]) & (position[None, :] < position[:, None])
    rank = jnp.sum(same.astype(jnp.int32), axis=1)
    target = (myself - shifts) % devices
    anchor = (myself + shifts) % devices
    store = b3_store.reshape(count, aux, size)
    mask = block_mask.reshape(count)
    chunks = chunk_groups(aux)
    widen = jnp.asarray(np.repeat(np.eye(BO, dtype=np.float32), 8, axis=1), BF)

    outgoing = [pack_blocks(store, target, rank, devices, capacity, groups) for groups in chunks]
    held = green[1]
    below, above = ring(held[:, mol_dev - HALF :], held[:, :HALF])
    outgoing[0], below, above = lax.optimization_barrier((outgoing[0], below, above))
    virtual, occupied = green_operands(green, below, above)
    incoming = []
    for c in range(len(chunks)):
        incoming.append(lax.all_to_all(outgoing[c], "row", split_axis=0, concat_axis=0, tiled=True))
        if c == 0:
            incoming[0], virtual, occupied = lax.optimization_barrier((incoming[0], virtual, occupied))
        if c + 1 < len(chunks):
            incoming[c], outgoing[c + 1] = lax.optimization_barrier((incoming[c], outgoing[c + 1]))
    parts, folded = [], []
    for c, groups in enumerate(chunks):
        if c:
            rank, folded[c - 1] = lax.optimization_barrier((rank, folded[c - 1]))
        own, first, last = spread_out(
            incoming[c], anchor, rank, mask, mol_dev, aux, capacity, groups
        )
        above_and_below = ring(last, first)
        parts.append((above_and_below[0], own, above_and_below[1]))
        folded.append(fold_kernel(own, virtual, occupied, widen))
    return chi_kernel(parts, folded, chunks, aux)


def solution(mesh):
    in_specs = (
        P(("groups", "row"), None, None, None),
        P("groups", None),
        P(None, None, ("groups", "row"), None, None),
        P(("groups", "row"), None),
    )
    out_specs = P(None, ("groups", "row"), None, None)
    return jax.shard_map(shards, mesh=mesh, in_specs=in_specs, out_specs=out_specs, check_vma=False)
```

```python
import functools

import jax
import jax.numpy as jnp
import numpy as np
from jax import lax
from jax.experimental import pallas as pl
from jax.experimental.pallas import tpu as pltpu
from jax.sharding import PartitionSpec as P

BO = 24
HALF = 2
NTAU = 2
NN = 5
NW = 9
LANE = 128
KEPT = 3
BF = jnp.bfloat16
F32 = jnp.float32
VMEM_LIMIT = 56 * 1024 * 1024


def call(body, name, grid, in_specs, out_specs, out_shape, scratch=(), prefetch=0):
    return pl.pallas_call(
        body,
        grid_spec=pltpu.PrefetchScalarGridSpec(
            num_scalar_prefetch=prefetch,
            grid=grid,
            in_specs=in_specs,
            out_specs=out_specs,
            scratch_shapes=list(scratch),
        ),
        out_shape=out_shape,
        name=name,
        compiler_params=pltpu.CompilerParams(vmem_limit_bytes=VMEM_LIMIT),
    )


def chunk_groups(aux):
    full = aux // 16
    last = [full] if aux % 16 else []
    return [list(range(full - 1)), [full - 1] + last]


def piece_rows(groups, aux):
    return [min(16, aux - 16 * g) for g in groups]


def piece_starts(groups, aux, halves):
    starts, row = [], 0
    for height in piece_rows(groups, aux):
        starts.append(row)
        row += height * halves
    return starts, row


def pack_blocks(store, target, rank, devices, capacity, groups):
    count, aux, size = store.shape
    pair = 2 if capacity > 1 else 1
    halves = (capacity + pair - 1) // pair
    heights = piece_rows(groups, aux)
    starts, total = piece_starts(groups, aux, halves)
    steps = 4
    batch = count // steps
    bulk = size // LANE * LANE
    rest = size - bulk

    def body(target_ref, rank_ref, *refs):
        out_ref = refs[-1]
        for i in range(batch):
            e = pl.program_id(0) * batch + i
            for r in range(halves * pair):

                @pl.when(rank_ref[e] == r)
                def _(i=i, e=e, r=r):
                    for ref, height, start in zip(refs, heights, starts):
                        first = start + (r // pair) * height
                        at = (target_ref[e], slice(first, first + height))
                        if r % pair:
                            out_ref[(*at, slice(size, size + rest))] = ref[i, :height, bulk:]
                            out_ref[(*at, slice(size + rest, None))] = ref[i, :height, :bulk]
                        else:
                            out_ref[(*at, slice(0, size))] = ref[i, :height]

    shape = (devices, total, pair * size)
    return call(
        body,
        "pack_blocks",
        (steps,),
        [pl.BlockSpec((batch, 16, size), lambda i, *_, g=g: (i, g, 0)) for g in groups],
        pl.BlockSpec(shape, lambda i, *_: (0, 0, 0)),
        jax.ShapeDtypeStruct(shape, BF),
        prefetch=2,
    )(target, rank, *([store] * len(groups)))


def regroup_tables(pair):
    size = BO * BO
    tables = []
    for at in range(0, size, LANE):
        width = min(LANE, size - at)
        first, last = at // BO, (at + width - 1) // BO
        table = np.zeros((NN, LANE, last - first + 1, LANE), np.float32)
        for lane in range(width):
            mu, i = divmod(at + lane, BO)
            for s in range(NN):
                table[s, lane, mu - first, s * BO + i] = 1
                if width < LANE and pair == 2:
                    table[s, lane + width, mu - first, s * BO + i] = 1
        tables.append((first, last, table.reshape(NN * LANE, -1)))
    return tables


def spread_out(incoming, source, rank, mask, aux, capacity, groups):
    size = BO * BO
    pair = 2 if capacity > 1 else 1
    halves = (capacity + pair - 1) // pair
    heights = piece_rows(groups, aux)
    starts, _ = piece_starts(groups, aux, halves)
    rows = 16 * len(groups)
    bulk = size // LANE * LANE
    rest = size - bulk
    tables = regroup_tables(pair)
    molecules = source.shape[0] // NN
    per_step = next(n for n in (6, 4, HALF) if molecules % n == 0)
    steps = molecules // per_step

    def body(source_ref, rank_ref, mask_ref, in_ref, *refs):
        table_refs = refs[: len(tables)]
        out_ref, first_ref, last_ref = refs[len(tables) :]
        step = pl.program_id(0)
        lane = lax.broadcasted_iota(jnp.int32, (16, LANE), 1)
        stretches = [[] for _ in tables]
        for i in range(per_step):
            a = step * per_step + i
            for height, start in zip(heights, starts):
                tiles = [[] for _ in tables]
                for s in range(NN):
                    e = a * NN + s
                    half, odd = rank_ref[e] // pair, rank_ref[e] % pair
                    if height == 16:
                        rows_at = pl.ds(pl.multiple_of(start + half * 16, 16), 16)
                        lanes_at = pl.ds(pl.multiple_of(odd * (size + rest), LANE), bulk)
                        main = in_ref[source_ref[e], rows_at, lanes_at]
                        tail = in_ref[source_ref[e], rows_at, bulk : bulk + pair * rest]
                    else:
                        both = in_ref[source_ref[e], start : start + halves * height, :].astype(F32)
                        picked = both[:height]
                        for h in range(1, halves):
                            picked = jnp.where(half == h, both[h * height : (h + 1) * height], picked)
                        gap = jnp.zeros((16 - height, picked.shape[1]), F32)
                        picked = jnp.concatenate([picked, gap], axis=0).astype(BF)
                        main, tail = picked[:, :bulk], picked[:, bulk : bulk + pair * rest]
                        if pair == 2:
                            main = jnp.where(odd == 1, picked[:, size + rest :], main)
                    kept = jnp.full((16, LANE), mask_ref[e], jnp.int32)
                    if pair == 2:
                        here = jnp.where((lane >= rest) == (odd == 1), kept, 0)
                    else:
                        here = kept
                        tail = jnp.concatenate([tail, jnp.zeros((16, LANE - rest), BF)], axis=1)
                    kept, here = kept.astype(F32).astype(BF), here.astype(F32).astype(BF)
                    for n in range(len(tables) - 1):
                        tiles[n].append(main[:, n * LANE : (n + 1) * LANE] * kept)
                    tiles[-1].append(tail * here)
                for n in range(len(tables)):
                    stretches[n].append(jnp.concatenate(tiles[n], axis=1))
        carried = None
        for n, (first, last, _) in enumerate(tables):
            moved = jnp.dot(
                jnp.concatenate(stretches[n], axis=0), table_refs[n][...], preferred_element_type=F32
            )
            shared = n + 1 < len(tables) and tables[n + 1][0] == last
            for mu in range(first, last + 1):
                tile = moved[:, (mu - first) * LANE : (mu - first + 1) * LANE]
                if mu == first and carried is not None:
                    tile = tile + carried
                if mu == last and shared:
                    carried = tile
                else:
                    out_ref[:, :, mu * LANE : (mu + 1) * LANE] = tile.astype(BF).reshape(
                        per_step, rows, LANE
                    )
            if not shared:
                carried = None

        @pl.when(step == 0)
        def _():
            first_ref[...] = out_ref[:HALF]

        @pl.when(step == steps - 1)
        def _():
            last_ref[...] = out_ref[per_step - HALF :]

    shape = (rows, BO * LANE)
    return call(
        body,
        "spread_out",
        (steps,),
        [pl.BlockSpec(incoming.shape, lambda a, *_: (0, 0, 0))]
        + [pl.BlockSpec(t.shape, lambda a, *_: (0, 0)) for _, _, t in tables],
        [
            pl.BlockSpec((per_step, *shape), lambda a, *_: (a, 0, 0)),
            pl.BlockSpec((HALF, *shape), lambda a, *_: (0, 0, 0)),
            pl.BlockSpec((HALF, *shape), lambda a, *_: (0, 0, 0)),
        ],
        [
            jax.ShapeDtypeStruct((molecules, *shape), BF),
            jax.ShapeDtypeStruct((HALF, *shape), BF),
            jax.ShapeDtypeStruct((HALF, *shape), BF),
        ],
        prefetch=3,
    )(source, rank, mask, incoming, *[jnp.asarray(t, BF) for _, _, t in tables])


def place_windows(virtual_ref, a, slots, window_ref):
    for t in range(NTAU):
        for s in range(NN):
            row = virtual_ref[a + s, t].astype(F32)
            for k, w in enumerate(slots):
                off = (s - w) * BO
                if off >= 0:
                    parts = [jnp.zeros((BO, off), F32)] * (off > 0) + [
                        row[:, : NN * BO - off],
                        jnp.zeros((BO, LANE - NN * BO), F32),
                    ]
                else:
                    parts = [row[:, -off:], jnp.zeros((BO, LANE - NN * BO - off), F32)]
                lanes = slice((t * KEPT + k) * LANE, (t * KEPT + k + 1) * LANE)
                window_ref[s * BO : (s + 1) * BO, lanes] = jnp.concatenate(parts, axis=1)


def join(refs, to_ref):
    at = 0
    for ref in refs:
        to_ref[at : at + ref.shape[0]] = ref[...]
        at += ref.shape[0]


def set_windows(u, a, virtual_ref, window_ref):
    @pl.when(u == 0)
    def _():
        window_ref[NN * BO :] = jnp.zeros((LANE - NN * BO, NTAU * KEPT * LANE), F32)

    @pl.when(u < HALF)
    def _():
        place_windows(virtual_ref, a, (0, 1, 1), window_ref)

    @pl.when(u >= HALF)
    def _():
        place_windows(virtual_ref, a, (2, 3, 4), window_ref)


def fold_unit(own, groups, window, occ_ref, widen, put):
    krons = []
    shape = (KEPT * BO, 8, BO * 8)
    keep = lax.broadcasted_iota(jnp.int32, shape[1:], 1) % 8 == lax.broadcasted_iota(jnp.int32, shape[1:], 0)
    keep = keep.astype(F32)[None]
    for t in range(NTAU):
        wide = jnp.dot(occ_ref[0, t], widen, preferred_element_type=F32)
        krons.append((wide[:, None, :] * keep).reshape(KEPT * BO * 8, BO * 8).astype(BF))
    part_rows = BO * 16 // 4
    for g in range(groups):
        rows = own(g)
        pieces = [[] for _ in range(NTAU * KEPT)]
        for p in range(0, NTAU * KEPT, 2):
            for first in range(0, BO * 16, part_rows):
                spread = jnp.dot(
                    rows[first : first + part_rows],
                    window[:, p * LANE : (p + 2) * LANE],
                    preferred_element_type=F32,
                )
                for z in range(2):
                    part = spread[:, z * LANE : (z + 1) * LANE].reshape(part_rows // 16, 2, 8, LANE)
                    part = [part[:, h].reshape(part_rows // 2, LANE) for h in range(2)]
                    pieces[p + z].append(jnp.concatenate(part, axis=1).astype(BF))
        for t in range(NTAU):
            for w in range(KEPT):
                part = jnp.concatenate(pieces[t * KEPT + w], axis=0)
                folded = jnp.dot(
                    krons[t][w * BO * 8 : (w + 1) * BO * 8], part, preferred_element_type=F32
                ).reshape(BO, 8, 2 * LANE)
                folded = jnp.concatenate([folded[:, :, :LANE], folded[:, :, LANE:]], axis=1).astype(BF)
                for el in range(BO):
                    put(w, t, g, el, folded[el])


def fold_kernel(own, virtual, occupied, widen):
    molecules, rows = own.shape[:2]
    units = occupied.shape[0]

    def body(own_ref, low_ref, mid_ref, high_ref, occ_ref, widen_ref, x_ref, window_ref, virtual_ref):
        u = pl.program_id(0)

        @pl.when(u == 0)
        def _():
            join((low_ref, mid_ref, high_ref), virtual_ref)

        set_windows(u, jnp.where(u < HALF, u, u - HALF), virtual_ref, window_ref)

        def rows_of(g):
            return jnp.concatenate(
                [
                    own_ref[0, g * 16 : (g + 1) * 16, mu * LANE : (mu + 1) * LANE]
                    for mu in range(BO)
                ],
                axis=0,
            )

        def put(w, t, g, el, tile):
            first = t * rows + g * 16
            x_ref[0, w, first : first + 16, el * LANE : (el + 1) * LANE] = tile

        fold_unit(rows_of, rows // 16, window_ref[...].astype(BF), occ_ref, widen_ref[...], put)

    whole = lambda x: pl.BlockSpec(x.shape, lambda u: (0,) * x.ndim)
    shape = (KEPT, NTAU * rows, BO * LANE)
    return call(
        body,
        "fold",
        (units,),
        [
            pl.BlockSpec((1, *own.shape[1:]), lambda u: (jnp.where(u < HALF, u, u - HALF), 0, 0)),
            *[whole(v) for v in virtual],
            pl.BlockSpec((1, *occupied.shape[1:]), lambda u: (u, 0, 0, 0)),
            whole(widen),
        ],
        pl.BlockSpec((1, *shape), lambda u: (u, 0, 0, 0)),
        jax.ShapeDtypeStruct((units, *shape), BF),
        [
            pltpu.VMEM((LANE, NTAU * KEPT * LANE), F32),
            pltpu.VMEM((units + HALF, NTAU, BO, NN * BO), BF),
        ],
    )(own, *virtual, occupied, widen)


def runs_of(groups):
    runs = []
    for at, g in enumerate(groups):
        if runs and runs[-1][1] + runs[-1][2] == g:
            runs[-1][2] += 1
        else:
            runs.append([at, g, 1])
    return runs


def row_plan(chunks):
    heights = [16 * len(groups) for groups in chunks]
    below = [NTAU * sum(heights[:c]) for c in range(len(chunks))]
    spots = sorted((g, c, at) for c, groups in enumerate(chunks) for at, g in enumerate(groups))
    plan = [[below[c] + t * heights[c] + at * 16 for _, c, at in spots] for t in range(NTAU)]
    return heights, below, plan


def in_order(result, plan):
    return [jnp.concatenate([result[at : at + 16] for at in spots], axis=0) for spots in plan]


def flatten(all_ref, at, count, rows, aux):
    return jnp.concatenate(
        [all_ref[at, pl.ds(p, count, stride=rows), :][:, :aux] for p in range(aux)], axis=1
    )


def chi_kernel(parts, folded, virtual, occupied, widen, chunks, aux):
    molecules = parts[0].shape[0]
    heights, below, plan = row_plan(chunks)
    rows = sum(heights)
    units = molecules + HALF
    head = 2
    ready = len(folded)
    moves = [
        (c, first, much, at * 16, g * 16, length * 16)
        for first, much in ((0, head), (head, molecules - head))
        for c, groups in enumerate(chunks)
        for at, g, length in runs_of(groups)
    ]

    def body(*refs):
        ins, xs = refs[: len(parts)], refs[len(parts) : len(parts) + ready]
        virtual_refs = refs[len(parts) + ready :][:3]
        occ_ref, widen_ref, out_ref, edge_ref = refs[len(parts) + ready + 3 :][:4]
        (blocks_ref, all_ref, x_ref, window_ref, virtual_ref, sem, x_sem, edge_sem) = refs[
            len(parts) + ready + 7 :
        ]
        q = pl.program_id(0)

        def loads(which):
            for i, (c, first, much, at, to, length) in enumerate(moves):
                if (first > 0) == which:
                    yield pltpu.make_async_copy(
                        ins[c].at[first : first + much, at : at + length],
                        blocks_ref.at[first : first + much, to : to + length],
                        sem.at[i],
                    )

        def fetch(step, c):
            return pltpu.make_async_copy(
                xs[c].at[step],
                x_ref.at[step % 4, :, below[c] : below[c] + NTAU * heights[c]],
                x_sem.at[c, step % 2],
            )

        def give(at, ring_at, k, i):
            return pltpu.make_async_copy(x_ref.at[ring_at, k], edge_ref.at[at], edge_sem.at[i])

        @pl.when(q == 0)
        def _():
            for copy in loads(False):
                copy.start()
            for c in range(ready):
                fetch(q, c).start()
            for copy in loads(True):
                copy.start()
            join(virtual_refs, virtual_ref)
            for copy in loads(False):
                copy.wait()

        @pl.when(q == HALF + head)
        def _():
            for copy in loads(True):
                copy.wait()

        @pl.when(q + 1 < units)
        def _():
            for c in range(ready):
                fetch(q + 1, c).start()

        @pl.when(q < units)
        def _():
            mine = jnp.where(q < HALF, q, q - HALF)
            set_windows(q, mine, virtual_ref, window_ref)
            last = chunks[-1]

            def rows_of(g):
                return jnp.concatenate(
                    [
                        blocks_ref[
                            mine, last[g] * 16 : (last[g] + 1) * 16, mu * LANE : (mu + 1) * LANE
                        ]
                        for mu in range(BO)
                    ],
                    axis=0,
                )

            def put(w, t, g, el, tile):
                first = below[-1] + t * heights[-1] + g * 16
                x_ref[q % 4, w, first : first + 16, el * LANE : (el + 1) * LANE] = tile

            fold_unit(rows_of, len(last), window_ref[...].astype(BF), occ_ref, widen_ref[...], put)
            for c in range(ready):
                fetch(q, c).wait()

        gifts = ((0, 0, 0), (0, 1, 1), (1, 2, 0), (units - 2, 3, 2), (units - 1, 4, 1), (units - 1, 5, 2))
        for i, (step, at, k) in enumerate(gifts):

            @pl.when(q == step)
            def _(i=i, step=step, at=at, k=k):
                give(at, step % 4, k, i).start()

        def chi(k):
            result = lax.dot_general(
                x_ref[(q + 4 - k) % 4, k], blocks_ref[q - HALF], (((1,), (1,)), ((), ())),
                preferred_element_type=F32,
            )
            return in_order(result, plan)

        def put_chi(back, w, values):
            ring_at = (q + 4 - back) % 4
            for t in range(NTAU):
                all_ref[ring_at, pl.ds((w * NTAU + t) * rows, rows), :rows] = values[t]

        def with_own():
            put_chi(0, 2, chi(0))

        def with_next():
            values = chi(1)
            put_chi(1, 3, values)
            put_chi(0, 1, [jnp.transpose(x) for x in values])

        def with_second():
            values = chi(2)
            put_chi(2, 4, values)
            put_chi(0, 0, [jnp.transpose(x) for x in values])

        def write():
            flat = flatten(all_ref, (q + 2) % 4, NN * NTAU, rows, aux)
            for w in range(NN):
                out_ref[0, w] = flat[w * NTAU : (w + 1) * NTAU]

        @pl.when(q == 2)
        def _():
            with_own()

        @pl.when(q == 3)
        def _():
            with_own()
            with_next()

        @pl.when((q >= 4) & (q < units))
        def _():
            with_own()
            with_next()
            with_second()
            write()

        @pl.when(q >= units)
        def _():
            write()

        for i, (step, at, k) in enumerate(gifts):

            @pl.when(q == step)
            def _(i=i, step=step, at=at, k=k):
                give(at, step % 4, k, i).wait()

    whole = lambda x: pl.BlockSpec(x.shape, lambda q: (0,) * x.ndim)
    x_shape = (NTAU * rows, BO * LANE)
    return call(
        body,
        "chi",
        (units + HALF,),
        [pl.BlockSpec(memory_space=pl.ANY)] * (len(parts) + ready)
        + [
            *[whole(v) for v in virtual],
            pl.BlockSpec((1, *occupied.shape[1:]), lambda q: (jnp.minimum(q, units - 1), 0, 0, 0)),
            whole(widen),
        ],
        [
            pl.BlockSpec((1, NN, NTAU, aux * aux), lambda q: (jnp.maximum(q - 2 * HALF, 0), 0, 0, 0)),
            pl.BlockSpec(memory_space=pl.ANY),
        ],
        [
            jax.ShapeDtypeStruct((molecules, NN, NTAU, aux * aux), F32),
            jax.ShapeDtypeStruct((6, *x_shape), BF),
        ],
        [
            pltpu.VMEM((molecules, rows, BO * LANE), BF),
            pltpu.VMEM((4, NN * NTAU * rows, LANE), F32),
            pltpu.VMEM((4, KEPT, *x_shape), BF),
            pltpu.VMEM((LANE, NTAU * KEPT * LANE), F32),
            pltpu.VMEM((units + HALF, NTAU, BO, NN * BO), BF),
            pltpu.SemaphoreType.DMA((len(moves),)),
            pltpu.SemaphoreType.DMA((max(ready, 1), 2)),
            pltpu.SemaphoreType.DMA((6,)),
        ],
    )(*parts, *folded, *virtual, occupied, widen)


def edge_kernel(chi, edge, halos, chunks, aux):
    molecules = chi.shape[0]
    heights, _, plan = row_plan(chunks)
    rows = sum(heights)
    place = np.array([[0, 0, 1, molecules - 2, molecules - 1, molecules - 1], [0, 1, 0, 4, 3, 4]], np.int32)
    spots = sorted((g, c, at) for c, groups in enumerate(chunks) for at, g in enumerate(groups))
    flat_halos = [h for side in halos for h in side]

    def body(edge_ref, *refs):
        below_refs, above_refs = refs[: len(chunks)], refs[len(chunks) : 2 * len(chunks)]
        out_ref, all_ref, flat_ref, sem = refs[2 * len(chunks) + 1 :]
        e = pl.program_id(0)

        def take(side, i):
            near = jnp.concatenate([side[c][i, at * 16 : (at + 1) * 16] for _, c, at in spots], axis=0)
            result = lax.dot_general(
                edge_ref[0], near, (((1,), (1,)), ((), ())), preferred_element_type=F32
            )
            for t, values in enumerate(in_order(result, plan)):
                all_ref[0, pl.ds((e * NTAU + t) * rows, rows), :rows] = values

        @pl.when(e < 3)
        def _():
            take(below_refs, jnp.minimum(e, 1))

        @pl.when(e >= 3)
        def _():
            take(above_refs, jnp.maximum(e - 4, 0))

        @pl.when(e == 5)
        def _():
            flat = flatten(all_ref, 0, 6 * NTAU, rows, aux)
            copies = []
            for i in range(6):
                flat_ref[i] = flat[i * NTAU : (i + 1) * NTAU]
                copies.append(
                    pltpu.make_async_copy(
                        flat_ref.at[i], out_ref.at[int(place[0, i]), int(place[1, i])], sem.at[i]
                    )
                )
                copies[-1].start()
            for copy in copies:
                copy.wait()

    return pl.pallas_call(
        body,
        grid=(6,),
        in_specs=[
            pl.BlockSpec((1, *edge.shape[1:]), lambda e: (e, 0, 0)),
            *[pl.BlockSpec(h.shape, lambda e: (0, 0, 0)) for h in flat_halos],
            pl.BlockSpec(memory_space=pl.ANY),
        ],
        out_specs=pl.BlockSpec(memory_space=pl.ANY),
        scratch_shapes=[
            pltpu.VMEM((1, 6 * NTAU * rows, LANE), F32),
            pltpu.VMEM((6, NTAU, aux * aux), F32),
            pltpu.SemaphoreType.DMA((6,)),
        ],
        out_shape=jax.ShapeDtypeStruct(chi.shape, F32),
        input_output_aliases={1 + len(flat_halos): 0},
        name="edge",
        compiler_params=pltpu.CompilerParams(vmem_limit_bytes=VMEM_LIMIT),
    )(edge, *flat_halos, chi)


def ring(low, high):
    count = lax.axis_size("row")
    up = [(i, (i + 1) % count) for i in range(count)]
    down = [(j, i) for i, j in up]
    return lax.ppermute(low, "row", up), lax.ppermute(high, "row", down)


def green_operands(green):
    mol_dev = green.shape[2]
    virtual = green[1].reshape(NTAU, mol_dev, NN, BO, BO)
    virtual = jnp.transpose(virtual, (1, 0, 3, 2, 4)).reshape(mol_dev, NTAU, BO, NN * BO)
    below, above = ring(virtual[mol_dev - HALF :], virtual[:HALF])
    occupied = green[0].reshape(NTAU, mol_dev, NN, BO, BO)
    first = occupied[:, :HALF]
    first = jnp.stack([first[:, :, 0], first[:, :, 1], first[:, :, 1]], axis=2)
    occupied = jnp.concatenate([first, occupied[:, :, HALF:]], axis=1)
    occupied = jnp.transpose(occupied, (1, 0, 2, 4, 3))
    return (below, virtual, above), occupied.reshape(mol_dev + HALF, NTAU, KEPT * BO, BO)


def shards(b3_store, block_shift, green, block_mask):
    devices = lax.axis_size("row")
    myself = lax.axis_index("row")
    mol_dev, _, aux, size = b3_store.shape
    count = mol_dev * NN
    capacity = (count + devices - 1) // devices
    pair = 2 if capacity > 1 else 1
    halves = (capacity + pair - 1) // pair
    shifts = block_shift.reshape(count)
    position = jnp.arange(count, dtype=jnp.int32)
    same = (shifts[:, None] == shifts[None, :]) & (position[None, :] < position[:, None])
    rank = jnp.sum(same.astype(jnp.int32), axis=1)
    target = (myself - shifts) % devices
    anchor = (myself + shifts) % devices
    store = b3_store.reshape(count, aux, size)
    mask = block_mask.reshape(count)
    chunks = chunk_groups(aux)
    widen = jnp.asarray(np.repeat(np.eye(BO, dtype=np.float32), 8, axis=1), BF)

    outgoing = [pack_blocks(store, target, rank, devices, capacity, groups) for groups in chunks]
    virtual, occupied = green_operands(green)
    arrived = lax.all_to_all(outgoing[0], "row", split_axis=0, concat_axis=0, tiled=True)
    arrived, virtual, occupied = lax.optimization_barrier((arrived, virtual, occupied))
    parts, folded, lows, highs = [], [], [], []
    for c, groups in enumerate(chunks):
        if c + 1 < len(chunks):
            arrived, sent, folded = lax.optimization_barrier((arrived, outgoing[c + 1], folded))
            coming = lax.all_to_all(sent, "row", split_axis=0, concat_axis=0, tiled=True)
        else:
            arrived, folded = lax.optimization_barrier((arrived, folded))
        own, first, last = spread_out(arrived, anchor, rank, mask, aux, capacity, groups)
        below, above = ring(last, first)
        parts.append(own)
        lows.append(below)
        highs.append(above)
        if c + 1 < len(chunks):
            folded = [*folded, fold_kernel(own, virtual, occupied, widen)]
            arrived = coming
    chi, edge = chi_kernel(parts, folded, virtual, occupied, widen, chunks, aux)
    chi = edge_kernel(chi, edge, (lows, highs), chunks, aux)
    return jnp.transpose(chi, (2, 0, 1, 3))


def solution(mesh):
    in_specs = (
        P(("groups", "row"), None, None, None),
        P("groups", None),
        P(None, None, ("groups", "row"), None, None),
        P(("groups", "row"), None),
    )
    out_specs = P(None, ("groups", "row"), None, None)
    return jax.shard_map(shards, mesh=mesh, in_specs=in_specs, out_specs=out_specs, check_vma=False)
```

```python
import functools

import jax
import jax.numpy as jnp
import numpy as np
from jax import lax
from jax.experimental import pallas as pl
from jax.experimental.pallas import tpu as pltpu
from jax.sharding import PartitionSpec as P

BO = 24
HALF = 2
NTAU = 2
NN = 5
NW = 9
LANE = 128
KEPT = 3
BF = jnp.bfloat16
F32 = jnp.float32
VMEM_LIMIT = 56 * 1024 * 1024


def call(body, name, grid, in_specs, out_specs, out_shape, scratch=(), prefetch=0):
    return pl.pallas_call(
        body,
        grid_spec=pltpu.PrefetchScalarGridSpec(
            num_scalar_prefetch=prefetch,
            grid=grid,
            in_specs=in_specs,
            out_specs=out_specs,
            scratch_shapes=list(scratch),
        ),
        out_shape=out_shape,
        name=name,
        compiler_params=pltpu.CompilerParams(vmem_limit_bytes=VMEM_LIMIT),
    )


def chunk_groups(aux):
    full = aux // 16
    last = [full] if aux % 16 else []
    return [list(range(full - 1)), [full - 1] + last]


def piece_rows(groups, aux):
    return [min(16, aux - 16 * g) for g in groups]


def piece_starts(groups, aux, halves):
    starts, row = [], 0
    for height in piece_rows(groups, aux):
        starts.append(row)
        row += height * halves
    return starts, row


def pack_blocks(store, target, rank, devices, capacity, groups):
    count, aux, size = store.shape
    pair = 2 if capacity > 1 else 1
    halves = (capacity + pair - 1) // pair
    heights = piece_rows(groups, aux)
    starts, total = piece_starts(groups, aux, halves)
    steps = 4
    batch = count // steps
    bulk = size // LANE * LANE
    rest = size - bulk

    def body(target_ref, rank_ref, *refs):
        out_ref = refs[-1]
        for i in range(batch):
            e = pl.program_id(0) * batch + i
            for r in range(halves * pair):

                @pl.when(rank_ref[e] == r)
                def _(i=i, e=e, r=r):
                    for ref, height, start in zip(refs, heights, starts):
                        first = start + (r // pair) * height
                        at = (target_ref[e], slice(first, first + height))
                        if r % pair:
                            out_ref[(*at, slice(size, size + rest))] = ref[i, :height, bulk:]
                            out_ref[(*at, slice(size + rest, None))] = ref[i, :height, :bulk]
                        else:
                            out_ref[(*at, slice(0, size))] = ref[i, :height]

    shape = (devices, total, pair * size)
    return call(
        body,
        "pack_blocks",
        (steps,),
        [pl.BlockSpec((batch, 16, size), lambda i, *_, g=g: (i, g, 0)) for g in groups],
        pl.BlockSpec(shape, lambda i, *_: (0, 0, 0)),
        jax.ShapeDtypeStruct(shape, BF),
        prefetch=2,
    )(target, rank, *([store] * len(groups)))


def regroup_tables(pair):
    size = BO * BO
    tables = []
    for at in range(0, size, LANE):
        width = min(LANE, size - at)
        first, last = at // BO, (at + width - 1) // BO
        table = np.zeros((NN, LANE, last - first + 1, LANE), np.float32)
        for lane in range(width):
            mu, i = divmod(at + lane, BO)
            for s in range(NN):
                table[s, lane, mu - first, s * BO + i] = 1
                if width < LANE and pair == 2:
                    table[s, lane + width, mu - first, s * BO + i] = 1
        tables.append((first, last, table.reshape(NN * LANE, -1)))
    return tables


def spread_out(incoming, source, rank, mask, aux, capacity, groups, ends):
    size = BO * BO
    pair = 2 if capacity > 1 else 1
    halves = (capacity + pair - 1) // pair
    heights = piece_rows(groups, aux)
    starts, _ = piece_starts(groups, aux, halves)
    rows = 16 * len(groups)
    bulk = size // LANE * LANE
    rest = size - bulk
    tables = regroup_tables(pair)
    molecules = source.shape[0] // NN
    per_step = next(n for n in (6, 4, HALF) if molecules % n == 0)
    steps = molecules // per_step
    held = ends[0].shape[1] if ends else 0

    def body(source_ref, rank_ref, mask_ref, in_ref, *refs):
        table_refs = refs[: len(tables)]
        end_refs = refs[len(tables) : len(tables) + len(ends)]
        out_ref, first_ref, last_ref = refs[len(tables) + len(ends) :]
        step = pl.program_id(0)
        lane = lax.broadcasted_iota(jnp.int32, (16, LANE), 1)
        stretches = [[] for _ in tables]
        for i in range(per_step):
            a = step * per_step + i
            for height, start in zip(heights, starts):
                tiles = [[] for _ in tables]
                for s in range(NN):
                    e = a * NN + s
                    half, odd = rank_ref[e] // pair, rank_ref[e] % pair
                    if height == 16:
                        rows_at = pl.ds(pl.multiple_of(start + half * 16, 16), 16)
                        lanes_at = pl.ds(pl.multiple_of(odd * (size + rest), LANE), bulk)
                        main = in_ref[source_ref[e], rows_at, lanes_at]
                        tail = in_ref[source_ref[e], rows_at, bulk : bulk + pair * rest]
                    else:
                        both = in_ref[source_ref[e], start : start + halves * height, :].astype(F32)
                        picked = both[:height]
                        for h in range(1, halves):
                            picked = jnp.where(half == h, both[h * height : (h + 1) * height], picked)
                        gap = jnp.zeros((16 - height, picked.shape[1]), F32)
                        picked = jnp.concatenate([picked, gap], axis=0).astype(BF)
                        main, tail = picked[:, :bulk], picked[:, bulk : bulk + pair * rest]
                        if pair == 2:
                            main = jnp.where(odd == 1, picked[:, size + rest :], main)
                    kept = jnp.full((16, LANE), mask_ref[e], jnp.int32)
                    if pair == 2:
                        here = jnp.where((lane >= rest) == (odd == 1), kept, 0)
                    else:
                        here = kept
                        tail = jnp.concatenate([tail, jnp.zeros((16, LANE - rest), BF)], axis=1)
                    kept, here = kept.astype(F32).astype(BF), here.astype(F32).astype(BF)
                    for n in range(len(tables) - 1):
                        tiles[n].append(main[:, n * LANE : (n + 1) * LANE] * kept)
                    tiles[-1].append(tail * here)
                for n in range(len(tables)):
                    stretches[n].append(jnp.concatenate(tiles[n], axis=1))
        carried = None
        for n, (first, last, _) in enumerate(tables):
            moved = jnp.dot(
                jnp.concatenate(stretches[n], axis=0), table_refs[n][...], preferred_element_type=F32
            )
            shared = n + 1 < len(tables) and tables[n + 1][0] == last
            for mu in range(first, last + 1):
                tile = moved[:, (mu - first) * LANE : (mu - first + 1) * LANE]
                if mu == first and carried is not None:
                    tile = tile + carried
                if mu == last and shared:
                    carried = tile
                else:
                    out_ref[:, :, mu * LANE : (mu + 1) * LANE] = tile.astype(BF).reshape(
                        per_step, rows, LANE
                    )
            if not shared:
                carried = None

        @pl.when(step == 0)
        def _():
            if ends:
                first_ref[:, :held] = end_refs[0][...]
            first_ref[:, held:] = out_ref[:HALF]

        @pl.when(step == steps - 1)
        def _():
            if ends:
                last_ref[:, :held] = end_refs[1][...]
            last_ref[:, held:] = out_ref[per_step - HALF :]

    shape = (rows, BO * LANE)
    end_shape = (HALF, held + rows, BO * LANE)
    return call(
        body,
        "spread_out",
        (steps,),
        [pl.BlockSpec(incoming.shape, lambda a, *_: (0, 0, 0))]
        + [pl.BlockSpec(t.shape, lambda a, *_: (0, 0)) for _, _, t in tables]
        + [pl.BlockSpec(x.shape, lambda a, *_: (0, 0, 0)) for x in ends],
        [
            pl.BlockSpec((per_step, *shape), lambda a, *_: (a, 0, 0)),
            pl.BlockSpec(end_shape, lambda a, *_: (0, 0, 0)),
            pl.BlockSpec(end_shape, lambda a, *_: (0, 0, 0)),
        ],
        [
            jax.ShapeDtypeStruct((molecules, *shape), BF),
            jax.ShapeDtypeStruct(end_shape, BF),
            jax.ShapeDtypeStruct(end_shape, BF),
        ],
        prefetch=3,
    )(source, rank, mask, incoming, *[jnp.asarray(t, BF) for _, _, t in tables], *ends)


def place_windows(virtual_ref, a, slots, window_ref):
    for t in range(NTAU):
        for s in range(NN):
            row = virtual_ref[a + s, t].astype(F32)
            for k, w in enumerate(slots):
                off = (s - w) * BO
                if off >= 0:
                    parts = [jnp.zeros((BO, off), F32)] * (off > 0) + [
                        row[:, : NN * BO - off],
                        jnp.zeros((BO, LANE - NN * BO), F32),
                    ]
                else:
                    parts = [row[:, -off:], jnp.zeros((BO, LANE - NN * BO - off), F32)]
                lanes = slice((t * KEPT + k) * LANE, (t * KEPT + k + 1) * LANE)
                window_ref[s * BO : (s + 1) * BO, lanes] = jnp.concatenate(parts, axis=1)


def join(refs, to_ref):
    at = 0
    for ref in refs:
        to_ref[at : at + ref.shape[0]] = ref[...]
        at += ref.shape[0]


def set_windows(u, a, virtual_ref, window_ref):
    @pl.when(u == 0)
    def _():
        window_ref[NN * BO :] = jnp.zeros((LANE - NN * BO, NTAU * KEPT * LANE), F32)

    @pl.when(u < HALF)
    def _():
        place_windows(virtual_ref, a, (0, 1, 1), window_ref)

    @pl.when(u >= HALF)
    def _():
        place_windows(virtual_ref, a, (2, 3, 4), window_ref)


def fold_unit(own, groups, window, occ_ref, widen, put):
    krons = []
    shape = (KEPT * BO, 8, BO * 8)
    keep = lax.broadcasted_iota(jnp.int32, shape[1:], 1) % 8 == lax.broadcasted_iota(jnp.int32, shape[1:], 0)
    keep = keep.astype(F32)[None]
    for t in range(NTAU):
        wide = jnp.dot(occ_ref[0, t], widen, preferred_element_type=F32)
        krons.append((wide[:, None, :] * keep).reshape(KEPT * BO * 8, BO * 8).astype(BF))
    part_rows = BO * 16 // 4
    for g in range(groups):
        rows = own(g)
        pieces = [[] for _ in range(NTAU * KEPT)]
        for p in range(0, NTAU * KEPT, 2):
            for first in range(0, BO * 16, part_rows):
                spread = jnp.dot(
                    rows[first : first + part_rows],
                    window[:, p * LANE : (p + 2) * LANE],
                    preferred_element_type=F32,
                )
                for z in range(2):
                    part = spread[:, z * LANE : (z + 1) * LANE].reshape(part_rows // 16, 2, 8, LANE)
                    part = [part[:, h].reshape(part_rows // 2, LANE) for h in range(2)]
                    pieces[p + z].append(jnp.concatenate(part, axis=1).astype(BF))
        for t in range(NTAU):
            for w in range(KEPT):
                part = jnp.concatenate(pieces[t * KEPT + w], axis=0)
                folded = jnp.dot(
                    krons[t][w * BO * 8 : (w + 1) * BO * 8], part, preferred_element_type=F32
                ).reshape(BO, 8, 2 * LANE)
                folded = jnp.concatenate([folded[:, :, :LANE], folded[:, :, LANE:]], axis=1).astype(BF)
                for el in range(BO):
                    put(w, t, g, el, folded[el])


def fold_kernel(own, virtual, occupied, widen):
    molecules, rows = own.shape[:2]
    units = occupied.shape[0]

    def body(own_ref, low_ref, mid_ref, high_ref, occ_ref, widen_ref, x_ref, window_ref, virtual_ref):
        u = pl.program_id(0)

        @pl.when(u == 0)
        def _():
            join((low_ref, mid_ref, high_ref), virtual_ref)

        set_windows(u, jnp.where(u < HALF, u, u - HALF), virtual_ref, window_ref)

        def rows_of(g):
            return jnp.concatenate(
                [
                    own_ref[0, g * 16 : (g + 1) * 16, mu * LANE : (mu + 1) * LANE]
                    for mu in range(BO)
                ],
                axis=0,
            )

        def put(w, t, g, el, tile):
            first = t * rows + g * 16
            x_ref[0, w, first : first + 16, el * LANE : (el + 1) * LANE] = tile

        fold_unit(rows_of, rows // 16, window_ref[...].astype(BF), occ_ref, widen_ref[...], put)

    whole = lambda x: pl.BlockSpec(x.shape, lambda u: (0,) * x.ndim)
    shape = (KEPT, NTAU * rows, BO * LANE)
    return call(
        body,
        "fold",
        (units,),
        [
            pl.BlockSpec((1, *own.shape[1:]), lambda u: (jnp.where(u < HALF, u, u - HALF), 0, 0)),
            *[whole(v) for v in virtual],
            pl.BlockSpec((1, *occupied.shape[1:]), lambda u: (u, 0, 0, 0)),
            whole(widen),
        ],
        pl.BlockSpec((1, *shape), lambda u: (u, 0, 0, 0)),
        jax.ShapeDtypeStruct((units, *shape), BF),
        [
            pltpu.VMEM((LANE, NTAU * KEPT * LANE), F32),
            pltpu.VMEM((units + HALF, NTAU, BO, NN * BO), BF),
        ],
    )(own, *virtual, occupied, widen)


def runs_of(groups):
    runs = []
    for at, g in enumerate(groups):
        if runs and runs[-1][1] + runs[-1][2] == g:
            runs[-1][2] += 1
        else:
            runs.append([at, g, 1])
    return runs


def row_plan(chunks):
    heights = [16 * len(groups) for groups in chunks]
    below = [NTAU * sum(heights[:c]) for c in range(len(chunks))]
    spots = sorted((g, c, at) for c, groups in enumerate(chunks) for at, g in enumerate(groups))
    plan = [[below[c] + t * heights[c] + at * 16 for _, c, at in spots] for t in range(NTAU)]
    return heights, below, plan


def in_order(result, plan):
    return [jnp.concatenate([result[at : at + 16] for at in spots], axis=0) for spots in plan]


def flatten(all_ref, at, count, rows, aux):
    return jnp.concatenate(
        [all_ref[at, pl.ds(p, count, stride=rows), :][:, :aux] for p in range(aux)], axis=1
    )


def chi_kernel(parts, folded, virtual, occupied, widen, chunks, aux):
    molecules = parts[0].shape[0]
    heights, below, plan = row_plan(chunks)
    rows = sum(heights)
    units = molecules + HALF
    head = 2
    ready = len(folded)
    moves = [
        (c, first, much, at * 16, g * 16, length * 16)
        for first, much in ((0, head), (head, molecules - head))
        for c, groups in enumerate(chunks)
        for at, g, length in runs_of(groups)
    ]

    def body(*refs):
        ins, xs = refs[: len(parts)], refs[len(parts) : len(parts) + ready]
        virtual_refs = refs[len(parts) + ready :][:3]
        occ_ref, widen_ref, out_ref, edge_ref = refs[len(parts) + ready + 3 :][:4]
        (blocks_ref, all_ref, x_ref, window_ref, virtual_ref, sem, x_sem, edge_sem) = refs[
            len(parts) + ready + 7 :
        ]
        q = pl.program_id(0)

        def loads(which):
            for i, (c, first, much, at, to, length) in enumerate(moves):
                if (first > 0) == which:
                    yield pltpu.make_async_copy(
                        ins[c].at[first : first + much, at : at + length],
                        blocks_ref.at[first : first + much, to : to + length],
                        sem.at[i],
                    )

        def fetch(step, c):
            return pltpu.make_async_copy(
                xs[c].at[step],
                x_ref.at[step % 4, :, below[c] : below[c] + NTAU * heights[c]],
                x_sem.at[c, step % 2],
            )

        def give(at, ring_at, k, i):
            return pltpu.make_async_copy(x_ref.at[ring_at, k], edge_ref.at[at], edge_sem.at[i])

        @pl.when(q == 0)
        def _():
            for copy in loads(False):
                copy.start()
            for c in range(ready):
                fetch(q, c).start()
            for copy in loads(True):
                copy.start()
            join(virtual_refs, virtual_ref)
            for copy in loads(False):
                copy.wait()

        @pl.when(q == HALF + head)
        def _():
            for copy in loads(True):
                copy.wait()

        @pl.when(q + 1 < units)
        def _():
            for c in range(ready):
                fetch(q + 1, c).start()

        @pl.when(q < units)
        def _():
            mine = jnp.where(q < HALF, q, q - HALF)
            set_windows(q, mine, virtual_ref, window_ref)
            last = chunks[-1]

            def rows_of(g):
                return jnp.concatenate(
                    [
                        blocks_ref[
                            mine, last[g] * 16 : (last[g] + 1) * 16, mu * LANE : (mu + 1) * LANE
                        ]
                        for mu in range(BO)
                    ],
                    axis=0,
                )

            def put(w, t, g, el, tile):
                first = below[-1] + t * heights[-1] + g * 16
                x_ref[q % 4, w, first : first + 16, el * LANE : (el + 1) * LANE] = tile

            fold_unit(rows_of, len(last), window_ref[...].astype(BF), occ_ref, widen_ref[...], put)
            for c in range(ready):
                fetch(q, c).wait()

        gifts = ((0, 0, 0), (0, 1, 1), (1, 2, 0), (units - 2, 3, 2), (units - 1, 4, 1), (units - 1, 5, 2))
        for i, (step, at, k) in enumerate(gifts):

            @pl.when(q == step)
            def _(i=i, step=step, at=at, k=k):
                give(at, step % 4, k, i).start()

        def chi(k):
            result = lax.dot_general(
                x_ref[(q + 4 - k) % 4, k], blocks_ref[q - HALF], (((1,), (1,)), ((), ())),
                preferred_element_type=F32,
            )
            return in_order(result, plan)

        def put_chi(back, w, values):
            ring_at = (q + 4 - back) % 4
            for t in range(NTAU):
                all_ref[ring_at, pl.ds((w * NTAU + t) * rows, rows), :rows] = values[t]

        def with_own():
            put_chi(0, 2, chi(0))

        def with_next():
            values = chi(1)
            put_chi(1, 3, values)
            put_chi(0, 1, [jnp.transpose(x) for x in values])

        def with_second():
            values = chi(2)
            put_chi(2, 4, values)
            put_chi(0, 0, [jnp.transpose(x) for x in values])

        def write():
            flat = flatten(all_ref, (q + 2) % 4, NN * NTAU, rows, aux)
            for w in range(NN):
                out_ref[0, w] = flat[w * NTAU : (w + 1) * NTAU]

        @pl.when(q == 2)
        def _():
            with_own()

        @pl.when(q == 3)
        def _():
            with_own()
            with_next()

        @pl.when((q >= 4) & (q < units))
        def _():
            with_own()
            with_next()
            with_second()
            write()

        @pl.when(q >= units)
        def _():
            write()

        for i, (step, at, k) in enumerate(gifts):

            @pl.when(q == step)
            def _(i=i, step=step, at=at, k=k):
                give(at, step % 4, k, i).wait()

    whole = lambda x: pl.BlockSpec(x.shape, lambda q: (0,) * x.ndim)
    x_shape = (NTAU * rows, BO * LANE)
    return call(
        body,
        "chi",
        (units + HALF,),
        [pl.BlockSpec(memory_space=pl.ANY)] * (len(parts) + ready)
        + [
            *[whole(v) for v in virtual],
            pl.BlockSpec((1, *occupied.shape[1:]), lambda q: (jnp.minimum(q, units - 1), 0, 0, 0)),
            whole(widen),
        ],
        [
            pl.BlockSpec((1, NN, NTAU, aux * aux), lambda q: (jnp.maximum(q - 2 * HALF, 0), 0, 0, 0)),
            pl.BlockSpec(memory_space=pl.ANY),
        ],
        [
            jax.ShapeDtypeStruct((molecules, NN, NTAU, aux * aux), F32),
            jax.ShapeDtypeStruct((6, *x_shape), BF),
        ],
        [
            pltpu.VMEM((molecules, rows, BO * LANE), BF),
            pltpu.VMEM((4, NN * NTAU * rows, LANE), F32),
            pltpu.VMEM((4, KEPT, *x_shape), BF),
            pltpu.VMEM((LANE, NTAU * KEPT * LANE), F32),
            pltpu.VMEM((units + HALF, NTAU, BO, NN * BO), BF),
            pltpu.SemaphoreType.DMA((len(moves),)),
            pltpu.SemaphoreType.DMA((max(ready, 1), 2)),
            pltpu.SemaphoreType.DMA((6,)),
        ],
    )(*parts, *folded, *virtual, occupied, widen)


def edge_kernel(chi, edge, below, above, chunks, aux):
    molecules = chi.shape[0]
    heights, _, plan = row_plan(chunks)
    rows = sum(heights)
    place = np.array([[0, 0, 1, molecules - 2, molecules - 1, molecules - 1], [0, 1, 0, 4, 3, 4]], np.int32)
    spots = sorted((g, c, at) for c, groups in enumerate(chunks) for at, g in enumerate(groups))
    starts = [sum(heights[:c]) for c in range(len(chunks))]

    def body(edge_ref, below_ref, above_ref, chi_ref, out_ref, all_ref, flat_ref, sem):
        e = pl.program_id(0)

        def take(side, i):
            tiles = [starts[c] + at * 16 for _, c, at in spots]
            near = jnp.concatenate([side[i, at : at + 16] for at in tiles], axis=0)
            result = lax.dot_general(
                edge_ref[0], near, (((1,), (1,)), ((), ())), preferred_element_type=F32
            )
            for t, values in enumerate(in_order(result, plan)):
                all_ref[0, pl.ds((e * NTAU + t) * rows, rows), :rows] = values

        @pl.when(e < 3)
        def _():
            take(below_ref, jnp.minimum(e, 1))

        @pl.when(e >= 3)
        def _():
            take(above_ref, jnp.maximum(e - 4, 0))

        @pl.when(e == 5)
        def _():
            flat = flatten(all_ref, 0, 6 * NTAU, rows, aux)
            copies = []
            for i in range(6):
                flat_ref[i] = flat[i * NTAU : (i + 1) * NTAU]
                copies.append(
                    pltpu.make_async_copy(
                        flat_ref.at[i], out_ref.at[int(place[0, i]), int(place[1, i])], sem.at[i]
                    )
                )
                copies[-1].start()
            for copy in copies:
                copy.wait()

    return pl.pallas_call(
        body,
        grid=(6,),
        in_specs=[
            pl.BlockSpec((1, *edge.shape[1:]), lambda e: (e, 0, 0)),
            pl.BlockSpec(below.shape, lambda e: (0, 0, 0)),
            pl.BlockSpec(above.shape, lambda e: (0, 0, 0)),
            pl.BlockSpec(memory_space=pl.ANY),
        ],
        out_specs=pl.BlockSpec(memory_space=pl.ANY),
        scratch_shapes=[
            pltpu.VMEM((1, 6 * NTAU * rows, LANE), F32),
            pltpu.VMEM((6, NTAU, aux * aux), F32),
            pltpu.SemaphoreType.DMA((6,)),
        ],
        out_shape=jax.ShapeDtypeStruct(chi.shape, F32),
        input_output_aliases={3: 0},
        name="edge",
        compiler_params=pltpu.CompilerParams(vmem_limit_bytes=VMEM_LIMIT),
    )(edge, below, above, chi)


def ring(low, high):
    count = lax.axis_size("row")
    up = [(i, (i + 1) % count) for i in range(count)]
    down = [(j, i) for i, j in up]
    return lax.ppermute(low, "row", up), lax.ppermute(high, "row", down)


def green_operands(green):
    mol_dev = green.shape[2]
    virtual = green[1].reshape(NTAU, mol_dev, NN, BO, BO)
    virtual = jnp.transpose(virtual, (1, 0, 3, 2, 4)).reshape(mol_dev, NTAU, BO, NN * BO)
    below, above = ring(virtual[mol_dev - HALF :], virtual[:HALF])
    occupied = green[0].reshape(NTAU, mol_dev, NN, BO, BO)
    first = occupied[:, :HALF]
    first = jnp.stack([first[:, :, 0], first[:, :, 1], first[:, :, 1]], axis=2)
    occupied = jnp.concatenate([first, occupied[:, :, HALF:]], axis=1)
    occupied = jnp.transpose(occupied, (1, 0, 2, 4, 3))
    return (below, virtual, above), occupied.reshape(mol_dev + HALF, NTAU, KEPT * BO, BO)


def shards(b3_store, block_shift, green, block_mask):
    devices = lax.axis_size("row")
    myself = lax.axis_index("row")
    mol_dev, _, aux, size = b3_store.shape
    count = mol_dev * NN
    capacity = (count + devices - 1) // devices
    pair = 2 if capacity > 1 else 1
    halves = (capacity + pair - 1) // pair
    shifts = block_shift.reshape(count)
    position = jnp.arange(count, dtype=jnp.int32)
    same = (shifts[:, None] == shifts[None, :]) & (position[None, :] < position[:, None])
    rank = jnp.sum(same.astype(jnp.int32), axis=1)
    target = (myself - shifts) % devices
    anchor = (myself + shifts) % devices
    store = b3_store.reshape(count, aux, size)
    mask = block_mask.reshape(count)
    chunks = chunk_groups(aux)
    widen = jnp.asarray(np.repeat(np.eye(BO, dtype=np.float32), 8, axis=1), BF)

    outgoing = [pack_blocks(store, target, rank, devices, capacity, groups) for groups in chunks]
    virtual, occupied = green_operands(green)
    arrived = lax.all_to_all(outgoing[0], "row", split_axis=0, concat_axis=0, tiled=True)
    arrived, virtual, occupied = lax.optimization_barrier((arrived, virtual, occupied))
    parts, folded, ends = [], [], []
    for c, groups in enumerate(chunks):
        if c + 1 < len(chunks):
            arrived, sent, folded = lax.optimization_barrier((arrived, outgoing[c + 1], folded))
            coming = lax.all_to_all(sent, "row", split_axis=0, concat_axis=0, tiled=True)
        else:
            arrived, folded = lax.optimization_barrier((arrived, folded))
        own, *ends = spread_out(arrived, anchor, rank, mask, aux, capacity, groups, ends)
        parts.append(own)
        if c + 1 < len(chunks):
            folded = [*folded, fold_kernel(own, virtual, occupied, widen)]
            arrived = coming
    below, above = ring(ends[1], ends[0])
    chi, edge = chi_kernel(parts, folded, virtual, occupied, widen, chunks, aux)
    chi = edge_kernel(chi, edge, below, above, chunks, aux)
    return jnp.transpose(chi, (2, 0, 1, 3))


def solution(mesh):
    in_specs = (
        P(("groups", "row"), None, None, None),
        P("groups", None),
        P(None, None, ("groups", "row"), None, None),
        P(("groups", "row"), None),
    )
    out_specs = P(None, ("groups", "row"), None, None)
    return jax.shard_map(shards, mesh=mesh, in_specs=in_specs, out_specs=out_specs, check_vma=False)
```

```python
import functools

import jax
import jax.numpy as jnp
import numpy as np
from jax import lax
from jax.experimental import pallas as pl
from jax.experimental.pallas import tpu as pltpu
from jax.sharding import PartitionSpec as P

BO = 24
HALF = 2
NTAU = 2
NN = 5
NW = 9
LANE = 128
KEPT = 3
BF = jnp.bfloat16
F32 = jnp.float32
MIB = 1024 * 1024
VMEM = {"pack_blocks": 56, "spread_out": 30, "fold": 44, "chi": 46, "edge": 16}


def call(body, name, grid, in_specs, out_specs, out_shape, scratch=(), prefetch=0):
    return pl.pallas_call(
        body,
        grid_spec=pltpu.PrefetchScalarGridSpec(
            num_scalar_prefetch=prefetch,
            grid=grid,
            in_specs=in_specs,
            out_specs=out_specs,
            scratch_shapes=list(scratch),
        ),
        out_shape=out_shape,
        name=name,
        compiler_params=pltpu.CompilerParams(vmem_limit_bytes=VMEM[name] * MIB),
    )


def chunk_groups(aux):
    full = aux // 16
    last = [full] if aux % 16 else []
    return [list(range(full - 1)), [full - 1] + last]


def piece_rows(groups, aux):
    return [min(16, aux - 16 * g) for g in groups]


def piece_starts(groups, aux, halves):
    starts, row = [], 0
    for height in piece_rows(groups, aux):
        starts.append(row)
        row += height * halves
    return starts, row


def pack_blocks(store, target, rank, devices, capacity, groups):
    count, aux, size = store.shape
    pair = 2 if capacity > 1 else 1
    halves = (capacity + pair - 1) // pair
    heights = piece_rows(groups, aux)
    starts, total = piece_starts(groups, aux, halves)
    steps = 4
    batch = count // steps
    bulk = size // LANE * LANE
    rest = size - bulk

    def body(target_ref, rank_ref, *refs):
        out_ref = refs[-1]
        for i in range(batch):
            e = pl.program_id(0) * batch + i
            for r in range(halves * pair):

                @pl.when(rank_ref[e] == r)
                def _(i=i, e=e, r=r):
                    for ref, height, start in zip(refs, heights, starts):
                        first = start + (r // pair) * height
                        at = (target_ref[e], slice(first, first + height))
                        if r % pair:
                            out_ref[(*at, slice(size, size + rest))] = ref[i, :height, bulk:]
                            out_ref[(*at, slice(size + rest, None))] = ref[i, :height, :bulk]
                        else:
                            out_ref[(*at, slice(0, size))] = ref[i, :height]

    shape = (devices, total, pair * size)
    return call(
        body,
        "pack_blocks",
        (steps,),
        [pl.BlockSpec((batch, 16, size), lambda i, *_, g=g: (i, g, 0)) for g in groups],
        pl.BlockSpec(shape, lambda i, *_: (0, 0, 0)),
        jax.ShapeDtypeStruct(shape, BF),
        prefetch=2,
    )(target, rank, *([store] * len(groups)))


def regroup_tables(pair):
    size = BO * BO
    tables = []
    for at in range(0, size, LANE):
        width = min(LANE, size - at)
        first, last = at // BO, (at + width - 1) // BO
        table = np.zeros((NN, LANE, last - first + 1, LANE), np.float32)
        for lane in range(width):
            mu, i = divmod(at + lane, BO)
            for s in range(NN):
                table[s, lane, mu - first, s * BO + i] = 1
                if width < LANE and pair == 2:
                    table[s, lane + width, mu - first, s * BO + i] = 1
        tables.append((first, last, table.reshape(NN * LANE, -1)))
    return tables


def spread_out(incoming, source, rank, mask, aux, capacity, groups, ends):
    size = BO * BO
    pair = 2 if capacity > 1 else 1
    halves = (capacity + pair - 1) // pair
    heights = piece_rows(groups, aux)
    starts, _ = piece_starts(groups, aux, halves)
    rows = 16 * len(groups)
    bulk = size // LANE * LANE
    rest = size - bulk
    tables = regroup_tables(pair)
    molecules = source.shape[0] // NN
    per_step = next(n for n in (6, 4, HALF) if molecules % n == 0)
    steps = molecules // per_step
    held = ends[0].shape[1] if ends else 0

    def body(source_ref, rank_ref, mask_ref, in_ref, *refs):
        table_refs = refs[: len(tables)]
        end_refs = refs[len(tables) : len(tables) + len(ends)]
        out_ref, first_ref, last_ref = refs[len(tables) + len(ends) :]
        step = pl.program_id(0)
        lane = lax.broadcasted_iota(jnp.int32, (16, LANE), 1)
        stretches = [[] for _ in tables]
        for i in range(per_step):
            a = step * per_step + i
            for height, start in zip(heights, starts):
                tiles = [[] for _ in tables]
                for s in range(NN):
                    e = a * NN + s
                    half, odd = rank_ref[e] // pair, rank_ref[e] % pair
                    if height == 16:
                        rows_at = pl.ds(pl.multiple_of(start + half * 16, 16), 16)
                        lanes_at = pl.ds(pl.multiple_of(odd * (size + rest), LANE), bulk)
                        main = in_ref[source_ref[e], rows_at, lanes_at]
                        tail = in_ref[source_ref[e], rows_at, bulk : bulk + pair * rest]
                    else:
                        both = in_ref[source_ref[e], start : start + halves * height, :].astype(F32)
                        picked = both[:height]
                        for h in range(1, halves):
                            picked = jnp.where(half == h, both[h * height : (h + 1) * height], picked)
                        gap = jnp.zeros((16 - height, picked.shape[1]), F32)
                        picked = jnp.concatenate([picked, gap], axis=0).astype(BF)
                        main, tail = picked[:, :bulk], picked[:, bulk : bulk + pair * rest]
                        if pair == 2:
                            main = jnp.where(odd == 1, picked[:, size + rest :], main)
                    kept = jnp.full((16, LANE), mask_ref[e], jnp.int32)
                    if pair == 2:
                        here = jnp.where((lane >= rest) == (odd == 1), kept, 0)
                    else:
                        here = kept
                        tail = jnp.concatenate([tail, jnp.zeros((16, LANE - rest), BF)], axis=1)
                    kept, here = kept.astype(F32).astype(BF), here.astype(F32).astype(BF)
                    for n in range(len(tables) - 1):
                        tiles[n].append(main[:, n * LANE : (n + 1) * LANE] * kept)
                    tiles[-1].append(tail * here)
                for n in range(len(tables)):
                    stretches[n].append(jnp.concatenate(tiles[n], axis=1))
        carried = None
        for n, (first, last, _) in enumerate(tables):
            moved = jnp.dot(
                jnp.concatenate(stretches[n], axis=0), table_refs[n][...], preferred_element_type=F32
            )
            shared = n + 1 < len(tables) and tables[n + 1][0] == last
            for mu in range(first, last + 1):
                tile = moved[:, (mu - first) * LANE : (mu - first + 1) * LANE]
                if mu == first and carried is not None:
                    tile = tile + carried
                if mu == last and shared:
                    carried = tile
                else:
                    out_ref[:, :, mu * LANE : (mu + 1) * LANE] = tile.astype(BF).reshape(
                        per_step, rows, LANE
                    )
            if not shared:
                carried = None

        @pl.when(step == 0)
        def _():
            if ends:
                first_ref[:, :held] = end_refs[0][...]
            first_ref[:, held:] = out_ref[:HALF]

        @pl.when(step == steps - 1)
        def _():
            if ends:
                last_ref[:, :held] = end_refs[1][...]
            last_ref[:, held:] = out_ref[per_step - HALF :]

    shape = (rows, BO * LANE)
    end_shape = (HALF, held + rows, BO * LANE)
    return call(
        body,
        "spread_out",
        (steps,),
        [pl.BlockSpec(incoming.shape, lambda a, *_: (0, 0, 0))]
        + [pl.BlockSpec(t.shape, lambda a, *_: (0, 0)) for _, _, t in tables]
        + [pl.BlockSpec(x.shape, lambda a, *_: (0, 0, 0)) for x in ends],
        [
            pl.BlockSpec((per_step, *shape), lambda a, *_: (a, 0, 0)),
            pl.BlockSpec(end_shape, lambda a, *_: (0, 0, 0)),
            pl.BlockSpec(end_shape, lambda a, *_: (0, 0, 0)),
        ],
        [
            jax.ShapeDtypeStruct((molecules, *shape), BF),
            jax.ShapeDtypeStruct(end_shape, BF),
            jax.ShapeDtypeStruct(end_shape, BF),
        ],
        prefetch=3,
    )(source, rank, mask, incoming, *[jnp.asarray(t, BF) for _, _, t in tables], *ends)


def place_windows(virtual_ref, a, slots, window_ref):
    for t in range(NTAU):
        for s in range(NN):
            row = virtual_ref[a + s, t].astype(F32)
            for k, w in enumerate(slots):
                off = (s - w) * BO
                if off >= 0:
                    parts = [jnp.zeros((BO, off), F32)] * (off > 0) + [
                        row[:, : NN * BO - off],
                        jnp.zeros((BO, LANE - NN * BO), F32),
                    ]
                else:
                    parts = [row[:, -off:], jnp.zeros((BO, LANE - NN * BO - off), F32)]
                lanes = slice((t * KEPT + k) * LANE, (t * KEPT + k + 1) * LANE)
                window_ref[s * BO : (s + 1) * BO, lanes] = jnp.concatenate(parts, axis=1)


def join(refs, to_ref):
    at = 0
    for ref in refs:
        to_ref[at : at + ref.shape[0]] = ref[...]
        at += ref.shape[0]


def set_windows(u, a, virtual_ref, window_ref):
    @pl.when(u == 0)
    def _():
        window_ref[NN * BO :] = jnp.zeros((LANE - NN * BO, NTAU * KEPT * LANE), F32)

    @pl.when(u < HALF)
    def _():
        place_windows(virtual_ref, a, (0, 1, 1), window_ref)

    @pl.when(u >= HALF)
    def _():
        place_windows(virtual_ref, a, (2, 3, 4), window_ref)


def fold_unit(own, groups, window, occ_ref, widen, put):
    krons = []
    shape = (KEPT * BO, 8, BO * 8)
    keep = lax.broadcasted_iota(jnp.int32, shape[1:], 1) % 8 == lax.broadcasted_iota(jnp.int32, shape[1:], 0)
    keep = keep.astype(F32)[None]
    for t in range(NTAU):
        wide = jnp.dot(occ_ref[0, t], widen, preferred_element_type=F32)
        krons.append((wide[:, None, :] * keep).reshape(KEPT * BO * 8, BO * 8).astype(BF))
    part_rows = BO * 16 // 4
    for g in range(groups):
        rows = own(g)
        pieces = [[] for _ in range(NTAU * KEPT)]
        for p in range(0, NTAU * KEPT, 2):
            for first in range(0, BO * 16, part_rows):
                spread = jnp.dot(
                    rows[first : first + part_rows],
                    window[:, p * LANE : (p + 2) * LANE],
                    preferred_element_type=F32,
                )
                for z in range(2):
                    part = spread[:, z * LANE : (z + 1) * LANE].reshape(part_rows // 16, 2, 8, LANE)
                    part = [part[:, h].reshape(part_rows // 2, LANE) for h in range(2)]
                    pieces[p + z].append(jnp.concatenate(part, axis=1).astype(BF))
        for t in range(NTAU):
            for w in range(KEPT):
                part = jnp.concatenate(pieces[t * KEPT + w], axis=0)
                folded = jnp.dot(
                    krons[t][w * BO * 8 : (w + 1) * BO * 8], part, preferred_element_type=F32
                ).reshape(BO, 8, 2 * LANE)
                folded = jnp.concatenate([folded[:, :, :LANE], folded[:, :, LANE:]], axis=1).astype(BF)
                for el in range(BO):
                    put(w, t, g, el, folded[el])


def fold_kernel(own, virtual, occupied, widen):
    molecules, rows = own.shape[:2]
    units = occupied.shape[0]

    def body(own_ref, low_ref, mid_ref, high_ref, occ_ref, widen_ref, x_ref, window_ref, virtual_ref):
        u = pl.program_id(0)

        @pl.when(u == 0)
        def _():
            join((low_ref, mid_ref, high_ref), virtual_ref)

        set_windows(u, jnp.where(u < HALF, u, u - HALF), virtual_ref, window_ref)

        def rows_of(g):
            return jnp.concatenate(
                [
                    own_ref[0, g * 16 : (g + 1) * 16, mu * LANE : (mu + 1) * LANE]
                    for mu in range(BO)
                ],
                axis=0,
            )

        def put(w, t, g, el, tile):
            first = t * rows + g * 16
            x_ref[0, w, first : first + 16, el * LANE : (el + 1) * LANE] = tile

        fold_unit(rows_of, rows // 16, window_ref[...].astype(BF), occ_ref, widen_ref[...], put)

    whole = lambda x: pl.BlockSpec(x.shape, lambda u: (0,) * x.ndim)
    shape = (KEPT, NTAU * rows, BO * LANE)
    return call(
        body,
        "fold",
        (units,),
        [
            pl.BlockSpec((1, *own.shape[1:]), lambda u: (jnp.where(u < HALF, u, u - HALF), 0, 0)),
            *[whole(v) for v in virtual],
            pl.BlockSpec((1, *occupied.shape[1:]), lambda u: (u, 0, 0, 0)),
            whole(widen),
        ],
        pl.BlockSpec((1, *shape), lambda u: (u, 0, 0, 0)),
        jax.ShapeDtypeStruct((units, *shape), BF),
        [
            pltpu.VMEM((LANE, NTAU * KEPT * LANE), F32),
            pltpu.VMEM((units + HALF, NTAU, BO, NN * BO), BF),
        ],
    )(own, *virtual, occupied, widen)


def runs_of(groups):
    runs = []
    for at, g in enumerate(groups):
        if runs and runs[-1][1] + runs[-1][2] == g:
            runs[-1][2] += 1
        else:
            runs.append([at, g, 1])
    return runs


def row_plan(chunks):
    heights = [16 * len(groups) for groups in chunks]
    below = [NTAU * sum(heights[:c]) for c in range(len(chunks))]
    spots = sorted((g, c, at) for c, groups in enumerate(chunks) for at, g in enumerate(groups))
    plan = [[below[c] + t * heights[c] + at * 16 for _, c, at in spots] for t in range(NTAU)]
    return heights, below, plan


def in_order(result, plan):
    return [jnp.concatenate([result[at : at + 16] for at in spots], axis=0) for spots in plan]


def flatten(all_ref, at, count, rows, aux):
    return jnp.concatenate(
        [all_ref[at, pl.ds(p, count, stride=rows), :][:, :aux] for p in range(aux)], axis=1
    )


def chi_kernel(parts, folded, virtual, occupied, widen, chunks, aux):
    molecules = parts[0].shape[0]
    heights, below, plan = row_plan(chunks)
    rows = sum(heights)
    units = molecules + HALF
    head = 2
    ready = len(folded)
    moves = [
        (c, first, much, at * 16, g * 16, length * 16)
        for first, much in ((0, head), (head, molecules - head))
        for c, groups in enumerate(chunks)
        for at, g, length in runs_of(groups)
    ]

    def body(*refs):
        ins, xs = refs[: len(parts)], refs[len(parts) : len(parts) + ready]
        virtual_refs = refs[len(parts) + ready :][:3]
        occ_ref, widen_ref, out_ref, edge_ref = refs[len(parts) + ready + 3 :][:4]
        (blocks_ref, all_ref, x_ref, window_ref, virtual_ref, sem, x_sem, edge_sem) = refs[
            len(parts) + ready + 7 :
        ]
        q = pl.program_id(0)

        def loads(which):
            for i, (c, first, much, at, to, length) in enumerate(moves):
                if (first > 0) == which:
                    yield pltpu.make_async_copy(
                        ins[c].at[first : first + much, at : at + length],
                        blocks_ref.at[first : first + much, to : to + length],
                        sem.at[i],
                    )

        def fetch(step, c):
            return pltpu.make_async_copy(
                xs[c].at[step],
                x_ref.at[step % 4, :, below[c] : below[c] + NTAU * heights[c]],
                x_sem.at[c, step % 2],
            )

        def give(at, ring_at, k, i):
            return pltpu.make_async_copy(x_ref.at[ring_at, k], edge_ref.at[at], edge_sem.at[i])

        @pl.when(q == 0)
        def _():
            for copy in loads(False):
                copy.start()
            for c in range(ready):
                fetch(q, c).start()
            for copy in loads(True):
                copy.start()
            join(virtual_refs, virtual_ref)
            for copy in loads(False):
                copy.wait()

        @pl.when(q == HALF + head)
        def _():
            for copy in loads(True):
                copy.wait()

        @pl.when(q + 1 < units)
        def _():
            for c in range(ready):
                fetch(q + 1, c).start()

        @pl.when(q < units)
        def _():
            mine = jnp.where(q < HALF, q, q - HALF)
            set_windows(q, mine, virtual_ref, window_ref)
            last = chunks[-1]

            def rows_of(g):
                return jnp.concatenate(
                    [
                        blocks_ref[
                            mine, last[g] * 16 : (last[g] + 1) * 16, mu * LANE : (mu + 1) * LANE
                        ]
                        for mu in range(BO)
                    ],
                    axis=0,
                )

            def put(w, t, g, el, tile):
                first = below[-1] + t * heights[-1] + g * 16
                x_ref[q % 4, w, first : first + 16, el * LANE : (el + 1) * LANE] = tile

            fold_unit(rows_of, len(last), window_ref[...].astype(BF), occ_ref, widen_ref[...], put)
            for c in range(ready):
                fetch(q, c).wait()

        gifts = ((0, 0, 0), (0, 1, 1), (1, 2, 0), (units - 2, 3, 2), (units - 1, 4, 1), (units - 1, 5, 2))
        for i, (step, at, k) in enumerate(gifts):

            @pl.when(q == step)
            def _(i=i, step=step, at=at, k=k):
                give(at, step % 4, k, i).start()

        def chi(k):
            result = lax.dot_general(
                x_ref[(q + 4 - k) % 4, k], blocks_ref[q - HALF], (((1,), (1,)), ((), ())),
                preferred_element_type=F32,
            )
            return in_order(result, plan)

        def put_chi(back, w, values):
            ring_at = (q + 4 - back) % 4
            for t in range(NTAU):
                all_ref[ring_at, pl.ds((w * NTAU + t) * rows, rows), :rows] = values[t]

        def with_own():
            put_chi(0, 2, chi(0))

        def with_next():
            values = chi(1)
            put_chi(1, 3, values)
            put_chi(0, 1, [jnp.transpose(x) for x in values])

        def with_second():
            values = chi(2)
            put_chi(2, 4, values)
            put_chi(0, 0, [jnp.transpose(x) for x in values])

        def write():
            flat = flatten(all_ref, (q + 2) % 4, NN * NTAU, rows, aux)
            for w in range(NN):
                out_ref[0, w] = flat[w * NTAU : (w + 1) * NTAU]

        @pl.when(q == 2)
        def _():
            with_own()

        @pl.when(q == 3)
        def _():
            with_own()
            with_next()

        @pl.when((q >= 4) & (q < units))
        def _():
            with_own()
            with_next()
            with_second()
            write()

        @pl.when(q >= units)
        def _():
            write()

        for i, (step, at, k) in enumerate(gifts):

            @pl.when(q == step)
            def _(i=i, step=step, at=at, k=k):
                give(at, step % 4, k, i).wait()

    whole = lambda x: pl.BlockSpec(x.shape, lambda q: (0,) * x.ndim)
    x_shape = (NTAU * rows, BO * LANE)
    return call(
        body,
        "chi",
        (units + HALF,),
        [pl.BlockSpec(memory_space=pl.ANY)] * (len(parts) + ready)
        + [
            *[whole(v) for v in virtual],
            pl.BlockSpec((1, *occupied.shape[1:]), lambda q: (jnp.minimum(q, units - 1), 0, 0, 0)),
            whole(widen),
        ],
        [
            pl.BlockSpec((1, NN, NTAU, aux * aux), lambda q: (jnp.maximum(q - 2 * HALF, 0), 0, 0, 0)),
            pl.BlockSpec(memory_space=pl.ANY),
        ],
        [
            jax.ShapeDtypeStruct((molecules, NN, NTAU, aux * aux), F32),
            jax.ShapeDtypeStruct((6, *x_shape), BF),
        ],
        [
            pltpu.VMEM((molecules, rows, BO * LANE), BF),
            pltpu.VMEM((4, NN * NTAU * rows, LANE), F32),
            pltpu.VMEM((4, KEPT, *x_shape), BF),
            pltpu.VMEM((LANE, NTAU * KEPT * LANE), F32),
            pltpu.VMEM((units + HALF, NTAU, BO, NN * BO), BF),
            pltpu.SemaphoreType.DMA((len(moves),)),
            pltpu.SemaphoreType.DMA((max(ready, 1), 2)),
            pltpu.SemaphoreType.DMA((6,)),
        ],
    )(*parts, *folded, *virtual, occupied, widen)


def edge_kernel(chi, edge, below, above, chunks, aux):
    molecules = chi.shape[0]
    heights, _, plan = row_plan(chunks)
    rows = sum(heights)
    place = np.array([[0, 0, 1, molecules - 2, molecules - 1, molecules - 1], [0, 1, 0, 4, 3, 4]], np.int32)
    spots = sorted((g, c, at) for c, groups in enumerate(chunks) for at, g in enumerate(groups))
    starts = [sum(heights[:c]) for c in range(len(chunks))]

    def body(edge_ref, below_ref, above_ref, chi_ref, out_ref, all_ref, flat_ref, sem):
        e = pl.program_id(0)

        def take(side, i):
            tiles = [starts[c] + at * 16 for _, c, at in spots]
            near = jnp.concatenate([side[i, at : at + 16] for at in tiles], axis=0)
            result = lax.dot_general(
                edge_ref[0], near, (((1,), (1,)), ((), ())), preferred_element_type=F32
            )
            for t, values in enumerate(in_order(result, plan)):
                all_ref[0, pl.ds((e * NTAU + t) * rows, rows), :rows] = values

        @pl.when(e < 3)
        def _():
            take(below_ref, jnp.minimum(e, 1))

        @pl.when(e >= 3)
        def _():
            take(above_ref, jnp.maximum(e - 4, 0))

        @pl.when(e == 5)
        def _():
            flat = flatten(all_ref, 0, 6 * NTAU, rows, aux)
            copies = []
            for i in range(6):
                flat_ref[i] = flat[i * NTAU : (i + 1) * NTAU]
                copies.append(
                    pltpu.make_async_copy(
                        flat_ref.at[i], out_ref.at[int(place[0, i]), int(place[1, i])], sem.at[i]
                    )
                )
                copies[-1].start()
            for copy in copies:
                copy.wait()

    return pl.pallas_call(
        body,
        grid=(6,),
        in_specs=[
            pl.BlockSpec((1, *edge.shape[1:]), lambda e: (e, 0, 0)),
            pl.BlockSpec(below.shape, lambda e: (0, 0, 0)),
            pl.BlockSpec(above.shape, lambda e: (0, 0, 0)),
            pl.BlockSpec(memory_space=pl.ANY),
        ],
        out_specs=pl.BlockSpec(memory_space=pl.ANY),
        scratch_shapes=[
            pltpu.VMEM((1, 6 * NTAU * rows, LANE), F32),
            pltpu.VMEM((6, NTAU, aux * aux), F32),
            pltpu.SemaphoreType.DMA((6,)),
        ],
        out_shape=jax.ShapeDtypeStruct(chi.shape, F32),
        input_output_aliases={3: 0},
        name="edge",
        compiler_params=pltpu.CompilerParams(vmem_limit_bytes=VMEM["edge"] * MIB),
    )(edge, below, above, chi)


def ring(low, high):
    count = lax.axis_size("row")
    up = [(i, (i + 1) % count) for i in range(count)]
    down = [(j, i) for i, j in up]
    return lax.ppermute(low, "row", up), lax.ppermute(high, "row", down)


def green_operands(green):
    mol_dev = green.shape[2]
    virtual = green[1].reshape(NTAU, mol_dev, NN, BO, BO)
    virtual = jnp.transpose(virtual, (1, 0, 3, 2, 4)).reshape(mol_dev, NTAU, BO, NN * BO)
    below, above = ring(virtual[mol_dev - HALF :], virtual[:HALF])
    occupied = green[0].reshape(NTAU, mol_dev, NN, BO, BO)
    first = occupied[:, :HALF]
    first = jnp.stack([first[:, :, 0], first[:, :, 1], first[:, :, 1]], axis=2)
    occupied = jnp.concatenate([first, occupied[:, :, HALF:]], axis=1)
    occupied = jnp.transpose(occupied, (1, 0, 2, 4, 3))
    return (below, virtual, above), occupied.reshape(mol_dev + HALF, NTAU, KEPT * BO, BO)


def shards(b3_store, block_shift, green, block_mask):
    devices = lax.axis_size("row")
    myself = lax.axis_index("row")
    mol_dev, _, aux, size = b3_store.shape
    count = mol_dev * NN
    capacity = (count + devices - 1) // devices
    pair = 2 if capacity > 1 else 1
    halves = (capacity + pair - 1) // pair
    shifts = block_shift.reshape(count)
    position = jnp.arange(count, dtype=jnp.int32)
    same = (shifts[:, None] == shifts[None, :]) & (position[None, :] < position[:, None])
    rank = jnp.sum(same.astype(jnp.int32), axis=1)
    target = (myself - shifts) % devices
    anchor = (myself + shifts) % devices
    store = b3_store.reshape(count, aux, size)
    mask = block_mask.reshape(count)
    chunks = chunk_groups(aux)
    widen = jnp.asarray(np.repeat(np.eye(BO, dtype=np.float32), 8, axis=1), BF)

    outgoing = [pack_blocks(store, target, rank, devices, capacity, groups) for groups in chunks]
    virtual, occupied = green_operands(green)
    arrived = lax.all_to_all(outgoing[0], "row", split_axis=0, concat_axis=0, tiled=True)
    arrived, virtual, occupied = lax.optimization_barrier((arrived, virtual, occupied))
    parts, folded, ends = [], [], []
    for c, groups in enumerate(chunks):
        if c + 1 < len(chunks):
            arrived, sent, folded = lax.optimization_barrier((arrived, outgoing[c + 1], folded))
            coming = lax.all_to_all(sent, "row", split_axis=0, concat_axis=0, tiled=True)
        else:
            arrived, folded = lax.optimization_barrier((arrived, folded))
        own, *ends = spread_out(arrived, anchor, rank, mask, aux, capacity, groups, ends)
        parts.append(own)
        if c + 1 < len(chunks):
            folded = [*folded, fold_kernel(own, virtual, occupied, widen)]
            arrived = coming
    below, above = ring(ends[1], ends[0])
    chi, edge = chi_kernel(parts, folded, virtual, occupied, widen, chunks, aux)
    chi = edge_kernel(chi, edge, below, above, chunks, aux)
    return jnp.transpose(chi, (2, 0, 1, 3))


def solution(mesh):
    in_specs = (
        P(("groups", "row"), None, None, None),
        P("groups", None),
        P(None, None, ("groups", "row"), None, None),
        P(("groups", "row"), None),
    )
    out_specs = P(None, ("groups", "row"), None, None)
    return jax.shard_map(shards, mesh=mesh, in_specs=in_specs, out_specs=out_specs, check_vma=False)
```

```python
import functools

import jax
import jax.numpy as jnp
import numpy as np
from jax import lax
from jax.experimental import pallas as pl
from jax.experimental.pallas import tpu as pltpu
from jax.sharding import PartitionSpec as P

BO = 24
HALF = 2
NTAU = 2
NN = 5
NW = 9
LANE = 128
KEPT = 3
BF = jnp.bfloat16
F32 = jnp.float32
MIB = 1024 * 1024
VMEM = {"pack_blocks": 56, "spread_out": 30, "fold": 40, "chi": 40, "edge": 16}


def call(body, name, grid, in_specs, out_specs, out_shape, scratch=(), prefetch=0):
    return pl.pallas_call(
        body,
        grid_spec=pltpu.PrefetchScalarGridSpec(
            num_scalar_prefetch=prefetch,
            grid=grid,
            in_specs=in_specs,
            out_specs=out_specs,
            scratch_shapes=list(scratch),
        ),
        out_shape=out_shape,
        name=name,
        compiler_params=pltpu.CompilerParams(vmem_limit_bytes=VMEM[name] * MIB),
    )


def chunk_groups(aux):
    full = aux // 16
    last = [full] if aux % 16 else []
    return [list(range(full - 1)), [full - 1] + last]


def piece_rows(groups, aux):
    return [min(16, aux - 16 * g) for g in groups]


def piece_starts(groups, aux, halves):
    starts, row = [], 0
    for height in piece_rows(groups, aux):
        starts.append(row)
        row += height * halves
    return starts, row


def pack_blocks(store, target, rank, devices, capacity, groups):
    count, aux, size = store.shape
    pair = 2 if capacity > 1 else 1
    halves = (capacity + pair - 1) // pair
    heights = piece_rows(groups, aux)
    starts, total = piece_starts(groups, aux, halves)
    steps = 4
    batch = count // steps
    bulk = size // LANE * LANE
    rest = size - bulk

    def body(target_ref, rank_ref, *refs):
        out_ref = refs[-1]
        for i in range(batch):
            e = pl.program_id(0) * batch + i
            for r in range(halves * pair):

                @pl.when(rank_ref[e] == r)
                def _(i=i, e=e, r=r):
                    for ref, height, start in zip(refs, heights, starts):
                        first = start + (r // pair) * height
                        at = (target_ref[e], slice(first, first + height))
                        if r % pair:
                            out_ref[(*at, slice(size, size + rest))] = ref[i, :height, bulk:]
                            out_ref[(*at, slice(size + rest, None))] = ref[i, :height, :bulk]
                        else:
                            out_ref[(*at, slice(0, size))] = ref[i, :height]

    shape = (devices, total, pair * size)
    return call(
        body,
        "pack_blocks",
        (steps,),
        [pl.BlockSpec((batch, 16, size), lambda i, *_, g=g: (i, g, 0)) for g in groups],
        pl.BlockSpec(shape, lambda i, *_: (0, 0, 0)),
        jax.ShapeDtypeStruct(shape, BF),
        prefetch=2,
    )(target, rank, *([store] * len(groups)))


def regroup_tables(pair):
    size = BO * BO
    tables = []
    for at in range(0, size, LANE):
        width = min(LANE, size - at)
        first, last = at // BO, (at + width - 1) // BO
        table = np.zeros((NN, LANE, last - first + 1, LANE), np.float32)
        for lane in range(width):
            mu, i = divmod(at + lane, BO)
            for s in range(NN):
                table[s, lane, mu - first, s * BO + i] = 1
                if width < LANE and pair == 2:
                    table[s, lane + width, mu - first, s * BO + i] = 1
        tables.append((first, last, table.reshape(NN * LANE, -1)))
    return tables


def spread_out(incoming, source, rank, mask, aux, capacity, groups, ends):
    size = BO * BO
    pair = 2 if capacity > 1 else 1
    halves = (capacity + pair - 1) // pair
    heights = piece_rows(groups, aux)
    starts, _ = piece_starts(groups, aux, halves)
    rows = 16 * len(groups)
    bulk = size // LANE * LANE
    rest = size - bulk
    tables = regroup_tables(pair)
    molecules = source.shape[0] // NN
    per_step = next(n for n in (6, 4, HALF) if molecules % n == 0)
    steps = molecules // per_step
    held = ends[0].shape[1] if ends else 0

    def body(source_ref, rank_ref, mask_ref, in_ref, *refs):
        table_refs = refs[: len(tables)]
        end_refs = refs[len(tables) : len(tables) + len(ends)]
        out_ref, first_ref, last_ref = refs[len(tables) + len(ends) :]
        step = pl.program_id(0)
        lane = lax.broadcasted_iota(jnp.int32, (16, LANE), 1)
        stretches = [[] for _ in tables]
        for i in range(per_step):
            a = step * per_step + i
            for height, start in zip(heights, starts):
                tiles = [[] for _ in tables]
                for s in range(NN):
                    e = a * NN + s
                    half, odd = rank_ref[e] // pair, rank_ref[e] % pair
                    if height == 16:
                        rows_at = pl.ds(pl.multiple_of(start + half * 16, 16), 16)
                        lanes_at = pl.ds(pl.multiple_of(odd * (size + rest), LANE), bulk)
                        main = in_ref[source_ref[e], rows_at, lanes_at]
                        tail = in_ref[source_ref[e], rows_at, bulk : bulk + pair * rest]
                    else:
                        both = in_ref[source_ref[e], start : start + halves * height, :].astype(F32)
                        picked = both[:height]
                        for h in range(1, halves):
                            picked = jnp.where(half == h, both[h * height : (h + 1) * height], picked)
                        gap = jnp.zeros((16 - height, picked.shape[1]), F32)
                        picked = jnp.concatenate([picked, gap], axis=0).astype(BF)
                        main, tail = picked[:, :bulk], picked[:, bulk : bulk + pair * rest]
                        if pair == 2:
                            main = jnp.where(odd == 1, picked[:, size + rest :], main)
                    kept = jnp.full((16, LANE), mask_ref[e], jnp.int32)
                    if pair == 2:
                        here = jnp.where((lane >= rest) == (odd == 1), kept, 0)
                    else:
                        here = kept
                        tail = jnp.concatenate([tail, jnp.zeros((16, LANE - rest), BF)], axis=1)
                    kept, here = kept.astype(F32).astype(BF), here.astype(F32).astype(BF)
                    for n in range(len(tables) - 1):
                        tiles[n].append(main[:, n * LANE : (n + 1) * LANE] * kept)
                    tiles[-1].append(tail * here)
                for n in range(len(tables)):
                    stretches[n].append(jnp.concatenate(tiles[n], axis=1))
        carried = None
        for n, (first, last, _) in enumerate(tables):
            moved = jnp.dot(
                jnp.concatenate(stretches[n], axis=0), table_refs[n][...], preferred_element_type=F32
            )
            shared = n + 1 < len(tables) and tables[n + 1][0] == last
            for mu in range(first, last + 1):
                tile = moved[:, (mu - first) * LANE : (mu - first + 1) * LANE]
                if mu == first and carried is not None:
                    tile = tile + carried
                if mu == last and shared:
                    carried = tile
                else:
                    out_ref[:, :, mu * LANE : (mu + 1) * LANE] = tile.astype(BF).reshape(
                        per_step, rows, LANE
                    )
            if not shared:
                carried = None

        @pl.when(step == 0)
        def _():
            if ends:
                first_ref[:, :held] = end_refs[0][...]
            first_ref[:, held:] = out_ref[:HALF]

        @pl.when(step == steps - 1)
        def _():
            if ends:
                last_ref[:, :held] = end_refs[1][...]
            last_ref[:, held:] = out_ref[per_step - HALF :]

    shape = (rows, BO * LANE)
    end_shape = (HALF, held + rows, BO * LANE)
    return call(
        body,
        "spread_out",
        (steps,),
        [pl.BlockSpec(incoming.shape, lambda a, *_: (0, 0, 0))]
        + [pl.BlockSpec(t.shape, lambda a, *_: (0, 0)) for _, _, t in tables]
        + [pl.BlockSpec(x.shape, lambda a, *_: (0, 0, 0)) for x in ends],
        [
            pl.BlockSpec((per_step, *shape), lambda a, *_: (a, 0, 0)),
            pl.BlockSpec(end_shape, lambda a, *_: (0, 0, 0)),
            pl.BlockSpec(end_shape, lambda a, *_: (0, 0, 0)),
        ],
        [
            jax.ShapeDtypeStruct((molecules, *shape), BF),
            jax.ShapeDtypeStruct(end_shape, BF),
            jax.ShapeDtypeStruct(end_shape, BF),
        ],
        prefetch=3,
    )(source, rank, mask, incoming, *[jnp.asarray(t, BF) for _, _, t in tables], *ends)


def place_windows(virtual_ref, a, slots, window_ref):
    for t in range(NTAU):
        for s in range(NN):
            row = virtual_ref[a + s, t].astype(F32)
            for k, w in enumerate(slots):
                off = (s - w) * BO
                if off >= 0:
                    parts = [jnp.zeros((BO, off), F32)] * (off > 0) + [
                        row[:, : NN * BO - off],
                        jnp.zeros((BO, LANE - NN * BO), F32),
                    ]
                else:
                    parts = [row[:, -off:], jnp.zeros((BO, LANE - NN * BO - off), F32)]
                lanes = slice((t * KEPT + k) * LANE, (t * KEPT + k + 1) * LANE)
                window_ref[s * BO : (s + 1) * BO, lanes] = jnp.concatenate(parts, axis=1)


def join(refs, to_ref):
    at = 0
    for ref in refs:
        to_ref[at : at + ref.shape[0]] = ref[...]
        at += ref.shape[0]


def set_windows(u, a, virtual_ref, window_ref):
    @pl.when(u == 0)
    def _():
        window_ref[NN * BO :] = jnp.zeros((LANE - NN * BO, NTAU * KEPT * LANE), F32)

    @pl.when(u < HALF)
    def _():
        place_windows(virtual_ref, a, (0, 1, 1), window_ref)

    @pl.when(u >= HALF)
    def _():
        place_windows(virtual_ref, a, (2, 3, 4), window_ref)


def fold_unit(own, groups, window, occ_ref, widen, put):
    krons = []
    shape = (KEPT * BO, 8, BO * 8)
    keep = lax.broadcasted_iota(jnp.int32, shape[1:], 1) % 8 == lax.broadcasted_iota(jnp.int32, shape[1:], 0)
    keep = keep.astype(F32)[None]
    for t in range(NTAU):
        wide = jnp.dot(occ_ref[0, t], widen, preferred_element_type=F32)
        krons.append((wide[:, None, :] * keep).reshape(KEPT * BO * 8, BO * 8).astype(BF))
    part_rows = BO * 16 // 4
    for g in range(groups):
        rows = own(g)
        pieces = [[] for _ in range(NTAU * KEPT)]
        for p in range(0, NTAU * KEPT, 2):
            for first in range(0, BO * 16, part_rows):
                spread = jnp.dot(
                    rows[first : first + part_rows],
                    window[:, p * LANE : (p + 2) * LANE],
                    preferred_element_type=F32,
                )
                for z in range(2):
                    part = spread[:, z * LANE : (z + 1) * LANE].reshape(part_rows // 16, 2, 8, LANE)
                    part = [part[:, h].reshape(part_rows // 2, LANE) for h in range(2)]
                    pieces[p + z].append(jnp.concatenate(part, axis=1).astype(BF))
        for t in range(NTAU):
            for w in range(KEPT):
                part = jnp.concatenate(pieces[t * KEPT + w], axis=0)
                folded = jnp.dot(
                    krons[t][w * BO * 8 : (w + 1) * BO * 8], part, preferred_element_type=F32
                ).reshape(BO, 8, 2 * LANE)
                folded = jnp.concatenate([folded[:, :, :LANE], folded[:, :, LANE:]], axis=1).astype(BF)
                for el in range(BO):
                    put(w, t, g, el, folded[el])


def fold_kernel(own, virtual, occupied, widen):
    molecules, rows = own.shape[:2]
    units = occupied.shape[0]

    def body(own_ref, low_ref, mid_ref, high_ref, occ_ref, widen_ref, x_ref, window_ref, virtual_ref):
        u = pl.program_id(0)

        @pl.when(u == 0)
        def _():
            join((low_ref, mid_ref, high_ref), virtual_ref)

        set_windows(u, jnp.where(u < HALF, u, u - HALF), virtual_ref, window_ref)

        def rows_of(g):
            return jnp.concatenate(
                [
                    own_ref[0, g * 16 : (g + 1) * 16, mu * LANE : (mu + 1) * LANE]
                    for mu in range(BO)
                ],
                axis=0,
            )

        def put(w, t, g, el, tile):
            first = t * rows + g * 16
            x_ref[0, w, first : first + 16, el * LANE : (el + 1) * LANE] = tile

        fold_unit(rows_of, rows // 16, window_ref[...].astype(BF), occ_ref, widen_ref[...], put)

    whole = lambda x: pl.BlockSpec(x.shape, lambda u: (0,) * x.ndim)
    shape = (KEPT, NTAU * rows, BO * LANE)
    return call(
        body,
        "fold",
        (units,),
        [
            pl.BlockSpec((1, *own.shape[1:]), lambda u: (jnp.where(u < HALF, u, u - HALF), 0, 0)),
            *[whole(v) for v in virtual],
            pl.BlockSpec((1, *occupied.shape[1:]), lambda u: (u, 0, 0, 0)),
            whole(widen),
        ],
        pl.BlockSpec((1, *shape), lambda u: (u, 0, 0, 0)),
        jax.ShapeDtypeStruct((units, *shape), BF),
        [
            pltpu.VMEM((LANE, NTAU * KEPT * LANE), F32),
            pltpu.VMEM((units + HALF, NTAU, BO, NN * BO), BF),
        ],
    )(own, *virtual, occupied, widen)


def runs_of(groups):
    runs = []
    for at, g in enumerate(groups):
        if runs and runs[-1][1] + runs[-1][2] == g:
            runs[-1][2] += 1
        else:
            runs.append([at, g, 1])
    return runs


def row_plan(chunks):
    heights = [16 * len(groups) for groups in chunks]
    below = [NTAU * sum(heights[:c]) for c in range(len(chunks))]
    spots = sorted((g, c, at) for c, groups in enumerate(chunks) for at, g in enumerate(groups))
    plan = [[below[c] + t * heights[c] + at * 16 for _, c, at in spots] for t in range(NTAU)]
    return heights, below, plan


def in_order(result, plan):
    return [jnp.concatenate([result[at : at + 16] for at in spots], axis=0) for spots in plan]


def flatten(all_ref, at, count, rows, aux):
    return jnp.concatenate(
        [all_ref[at, pl.ds(p, count, stride=rows), :][:, :aux] for p in range(aux)], axis=1
    )


def chi_kernel(parts, folded, virtual, occupied, widen, chunks, aux):
    molecules = parts[0].shape[0]
    heights, below, plan = row_plan(chunks)
    rows = sum(heights)
    units = molecules + HALF
    head = 2
    ready = len(folded)
    moves = [
        (c, first, much, at * 16, g * 16, length * 16)
        for first, much in ((0, head), (head, molecules - head))
        for c, groups in enumerate(chunks)
        for at, g, length in runs_of(groups)
    ]

    def body(*refs):
        ins, xs = refs[: len(parts)], refs[len(parts) : len(parts) + ready]
        virtual_refs = refs[len(parts) + ready :][:3]
        occ_ref, widen_ref, out_ref, edge_ref = refs[len(parts) + ready + 3 :][:4]
        (blocks_ref, all_ref, x_ref, window_ref, virtual_ref, sem, x_sem, edge_sem) = refs[
            len(parts) + ready + 7 :
        ]
        q = pl.program_id(0)

        def loads(which):
            for i, (c, first, much, at, to, length) in enumerate(moves):
                if (first > 0) == which:
                    yield pltpu.make_async_copy(
                        ins[c].at[first : first + much, at : at + length],
                        blocks_ref.at[first : first + much, to : to + length],
                        sem.at[i],
                    )

        def fetch(step, c):
            return pltpu.make_async_copy(
                xs[c].at[step],
                x_ref.at[step % 4, :, below[c] : below[c] + NTAU * heights[c]],
                x_sem.at[c, step % 2],
            )

        def give(at, ring_at, k, i):
            return pltpu.make_async_copy(x_ref.at[ring_at, k], edge_ref.at[at], edge_sem.at[i])

        @pl.when(q == 0)
        def _():
            for copy in loads(False):
                copy.start()
            for c in range(ready):
                fetch(q, c).start()
            for copy in loads(True):
                copy.start()
            join(virtual_refs, virtual_ref)
            for copy in loads(False):
                copy.wait()

        @pl.when(q == HALF + head)
        def _():
            for copy in loads(True):
                copy.wait()

        @pl.when(q + 1 < units)
        def _():
            for c in range(ready):
                fetch(q + 1, c).start()

        @pl.when(q < units)
        def _():
            mine = jnp.where(q < HALF, q, q - HALF)
            set_windows(q, mine, virtual_ref, window_ref)
            last = chunks[-1]

            def rows_of(g):
                return jnp.concatenate(
                    [
                        blocks_ref[
                            mine, last[g] * 16 : (last[g] + 1) * 16, mu * LANE : (mu + 1) * LANE
                        ]
                        for mu in range(BO)
                    ],
                    axis=0,
                )

            def put(w, t, g, el, tile):
                first = below[-1] + t * heights[-1] + g * 16
                x_ref[q % 4, w, first : first + 16, el * LANE : (el + 1) * LANE] = tile

            fold_unit(rows_of, len(last), window_ref[...].astype(BF), occ_ref, widen_ref[...], put)
            for c in range(ready):
                fetch(q, c).wait()

        gifts = ((0, 0, 0), (0, 1, 1), (1, 2, 0), (units - 2, 3, 2), (units - 1, 4, 1), (units - 1, 5, 2))
        for i, (step, at, k) in enumerate(gifts):

            @pl.when(q == step)
            def _(i=i, step=step, at=at, k=k):
                give(at, step % 4, k, i).start()

        def chi(k):
            result = lax.dot_general(
                x_ref[(q + 4 - k) % 4, k], blocks_ref[q - HALF], (((1,), (1,)), ((), ())),
                preferred_element_type=F32,
            )
            return in_order(result, plan)

        def put_chi(back, w, values):
            ring_at = (q + 4 - back) % 4
            for t in range(NTAU):
                all_ref[ring_at, pl.ds((w * NTAU + t) * rows, rows), :rows] = values[t]

        def with_own():
            put_chi(0, 2, chi(0))

        def with_next():
            values = chi(1)
            put_chi(1, 3, values)
            put_chi(0, 1, [jnp.transpose(x) for x in values])

        def with_second():
            values = chi(2)
            put_chi(2, 4, values)
            put_chi(0, 0, [jnp.transpose(x) for x in values])

        def write():
            flat = flatten(all_ref, (q + 2) % 4, NN * NTAU, rows, aux)
            for w in range(NN):
                out_ref[0, w] = flat[w * NTAU : (w + 1) * NTAU]

        @pl.when(q == 2)
        def _():
            with_own()

        @pl.when(q == 3)
        def _():
            with_own()
            with_next()

        @pl.when((q >= 4) & (q < units))
        def _():
            with_own()
            with_next()
            with_second()
            write()

        @pl.when(q >= units)
        def _():
            write()

        for i, (step, at, k) in enumerate(gifts):

            @pl.when(q == step)
            def _(i=i, step=step, at=at, k=k):
                give(at, step % 4, k, i).wait()

    whole = lambda x: pl.BlockSpec(x.shape, lambda q: (0,) * x.ndim)
    x_shape = (NTAU * rows, BO * LANE)
    return call(
        body,
        "chi",
        (units + HALF,),
        [pl.BlockSpec(memory_space=pl.ANY)] * (len(parts) + ready)
        + [
            *[whole(v) for v in virtual],
            pl.BlockSpec((1, *occupied.shape[1:]), lambda q: (jnp.minimum(q, units - 1), 0, 0, 0)),
            whole(widen),
        ],
        [
            pl.BlockSpec((1, NN, NTAU, aux * aux), lambda q: (jnp.maximum(q - 2 * HALF, 0), 0, 0, 0)),
            pl.BlockSpec(memory_space=pl.ANY),
        ],
        [
            jax.ShapeDtypeStruct((molecules, NN, NTAU, aux * aux), F32),
            jax.ShapeDtypeStruct((6, *x_shape), BF),
        ],
        [
            pltpu.VMEM((molecules, rows, BO * LANE), BF),
            pltpu.VMEM((4, NN * NTAU * rows, LANE), F32),
            pltpu.VMEM((4, KEPT, *x_shape), BF),
            pltpu.VMEM((LANE, NTAU * KEPT * LANE), F32),
            pltpu.VMEM((units + HALF, NTAU, BO, NN * BO), BF),
            pltpu.SemaphoreType.DMA((len(moves),)),
            pltpu.SemaphoreType.DMA((max(ready, 1), 2)),
            pltpu.SemaphoreType.DMA((6,)),
        ],
    )(*parts, *folded, *virtual, occupied, widen)


def edge_kernel(chi, edge, below, above, chunks, aux):
    molecules = chi.shape[0]
    heights, _, plan = row_plan(chunks)
    rows = sum(heights)
    place = np.array([[0, 0, 1, molecules - 2, molecules - 1, molecules - 1], [0, 1, 0, 4, 3, 4]], np.int32)
    spots = sorted((g, c, at) for c, groups in enumerate(chunks) for at, g in enumerate(groups))
    starts = [sum(heights[:c]) for c in range(len(chunks))]

    def body(edge_ref, below_ref, above_ref, chi_ref, out_ref, all_ref, flat_ref, sem):
        e = pl.program_id(0)

        def take(side, i):
            tiles = [starts[c] + at * 16 for _, c, at in spots]
            near = jnp.concatenate([side[i, at : at + 16] for at in tiles], axis=0)
            result = lax.dot_general(
                edge_ref[0], near, (((1,), (1,)), ((), ())), preferred_element_type=F32
            )
            for t, values in enumerate(in_order(result, plan)):
                all_ref[0, pl.ds((e * NTAU + t) * rows, rows), :rows] = values

        @pl.when(e < 3)
        def _():
            take(below_ref, jnp.minimum(e, 1))

        @pl.when(e >= 3)
        def _():
            take(above_ref, jnp.maximum(e - 4, 0))

        @pl.when(e == 5)
        def _():
            flat = flatten(all_ref, 0, 6 * NTAU, rows, aux)
            copies = []
            for i in range(6):
                flat_ref[i] = flat[i * NTAU : (i + 1) * NTAU]
                copies.append(
                    pltpu.make_async_copy(
                        flat_ref.at[i], out_ref.at[int(place[0, i]), int(place[1, i])], sem.at[i]
                    )
                )
                copies[-1].start()
            for copy in copies:
                copy.wait()

    return pl.pallas_call(
        body,
        grid=(6,),
        in_specs=[
            pl.BlockSpec((1, *edge.shape[1:]), lambda e: (e, 0, 0)),
            pl.BlockSpec(below.shape, lambda e: (0, 0, 0)),
            pl.BlockSpec(above.shape, lambda e: (0, 0, 0)),
            pl.BlockSpec(memory_space=pl.ANY),
        ],
        out_specs=pl.BlockSpec(memory_space=pl.ANY),
        scratch_shapes=[
            pltpu.VMEM((1, 6 * NTAU * rows, LANE), F32),
            pltpu.VMEM((6, NTAU, aux * aux), F32),
            pltpu.SemaphoreType.DMA((6,)),
        ],
        out_shape=jax.ShapeDtypeStruct(chi.shape, F32),
        input_output_aliases={3: 0},
        name="edge",
        compiler_params=pltpu.CompilerParams(vmem_limit_bytes=VMEM["edge"] * MIB),
    )(edge, below, above, chi)


def ring(low, high):
    count = lax.axis_size("row")
    up = [(i, (i + 1) % count) for i in range(count)]
    down = [(j, i) for i, j in up]
    return lax.ppermute(low, "row", up), lax.ppermute(high, "row", down)


def green_operands(green):
    mol_dev = green.shape[2]
    virtual = green[1].reshape(NTAU, mol_dev, NN, BO, BO)
    virtual = jnp.transpose(virtual, (1, 0, 3, 2, 4)).reshape(mol_dev, NTAU, BO, NN * BO)
    below, above = ring(virtual[mol_dev - HALF :], virtual[:HALF])
    occupied = green[0].reshape(NTAU, mol_dev, NN, BO, BO)
    first = occupied[:, :HALF]
    first = jnp.stack([first[:, :, 0], first[:, :, 1], first[:, :, 1]], axis=2)
    occupied = jnp.concatenate([first, occupied[:, :, HALF:]], axis=1)
    occupied = jnp.transpose(occupied, (1, 0, 2, 4, 3))
    return (below, virtual, above), occupied.reshape(mol_dev + HALF, NTAU, KEPT * BO, BO)


def shards(b3_store, block_shift, green, block_mask):
    devices = lax.axis_size("row")
    myself = lax.axis_index("row")
    mol_dev, _, aux, size = b3_store.shape
    count = mol_dev * NN
    capacity = (count + devices - 1) // devices
    pair = 2 if capacity > 1 else 1
    halves = (capacity + pair - 1) // pair
    shifts = block_shift.reshape(count)
    position = jnp.arange(count, dtype=jnp.int32)
    same = (shifts[:, None] == shifts[None, :]) & (position[None, :] < position[:, None])
    rank = jnp.sum(same.astype(jnp.int32), axis=1)
    target = (myself - shifts) % devices
    anchor = (myself + shifts) % devices
    store = b3_store.reshape(count, aux, size)
    mask = block_mask.reshape(count)
    chunks = chunk_groups(aux)
    widen = jnp.asarray(np.repeat(np.eye(BO, dtype=np.float32), 8, axis=1), BF)

    outgoing = [pack_blocks(store, target, rank, devices, capacity, groups) for groups in chunks]
    virtual, occupied = green_operands(green)
    arrived = lax.all_to_all(outgoing[0], "row", split_axis=0, concat_axis=0, tiled=True)
    arrived, virtual, occupied = lax.optimization_barrier((arrived, virtual, occupied))
    parts, folded, ends = [], [], []
    for c, groups in enumerate(chunks):
        if c + 1 < len(chunks):
            arrived, sent, folded = lax.optimization_barrier((arrived, outgoing[c + 1], folded))
            coming = lax.all_to_all(sent, "row", split_axis=0, concat_axis=0, tiled=True)
        else:
            arrived, folded = lax.optimization_barrier((arrived, folded))
        own, *ends = spread_out(arrived, anchor, rank, mask, aux, capacity, groups, ends)
        parts.append(own)
        if c + 1 < len(chunks):
            folded = [*folded, fold_kernel(own, virtual, occupied, widen)]
            arrived = coming
    below, above = ring(ends[1], ends[0])
    chi, edge = chi_kernel(parts, folded, virtual, occupied, widen, chunks, aux)
    chi = edge_kernel(chi, edge, below, above, chunks, aux)
    return jnp.transpose(chi, (2, 0, 1, 3))


def solution(mesh):
    in_specs = (
        P(("groups", "row"), None, None, None),
        P("groups", None),
        P(None, None, ("groups", "row"), None, None),
        P(("groups", "row"), None),
    )
    out_specs = P(None, ("groups", "row"), None, None)
    return jax.shard_map(shards, mesh=mesh, in_specs=in_specs, out_specs=out_specs, check_vma=False)
```
